128 devices in a mesh: src: 8 (over x, z_hi), tgt: 16 (over y, z_lo, core).
Axes of the slice: x: 4, y: 4, z: 4 (z_hi: 2, z_lo: 2; z = z_hi * 2 + z_lo), core: 2. Of those that a mesh axis runs over, the one named last changes fastest.
Arguments:
- noise: bfloat16 [4096, 2048], P(('src', 'tgt')), may hold values from -6 to 6
- data: bfloat16 [4096, 2048], P(('src', 'tgt')), may hold values from -6 to 6
- t_index: int32 [4096], P(('src', 'tgt')), may hold values from 0 to 1000
- embed_weight: bfloat16 [64, 2048], replicated, may hold values from -0.75 to 0.75
- position: bfloat16 [32, 2048], replicated, may hold values from -6 to 6
- norm_gain: float32 [2048], replicated, may hold values from 0.5 to 1.5
- qkv_weight: bfloat16 [2048, 6144], P(None, 'tgt'), may hold values from -0.125 to 0.125
Outputs:
- velocity: bfloat16 [4096, 2048], P(('src', 'tgt'))
- qkv: bfloat16 [131072, 6144], P(('src', 'tgt'))
The draws below stay inside these ranges and needn't reach their ends.
All inputs are finite; a program needn't handle non-finite values.
Results may differ from the reference program's by a relative error of at most 0.014.
Values may be sent and summed in bfloat16 or wider, within the bound.
No kernel may reach another device: no remote copies, remote signals or barrier semaphores. Data moves between devices by JAX's collectives and lax.ppermute only.
A program may use at most 448 MiB of HBM per device.

```python
import jax
import jax.numpy as jnp
from jax import lax

WIDTH = 2048
PATCH_IN = 64
NPATCH = 32
ITERS = 3
TGRID = 1000
LATENT = 2048
QKV = 6144
BATCH = 4096


def latent_data(key):
    base = jax.random.normal(jax.random.fold_in(key, 11), (BATCH, LATENT), jnp.float32)
    return jnp.clip(base, -6.0, 6.0)


def draw_data(key, part):
    return latent_data(key).astype(jnp.bfloat16)


def draw_noise(key, part):
    fresh = jax.random.normal(jax.random.fold_in(key, 12), (BATCH, LATENT), jnp.float32)
    return jnp.clip(fresh, -6.0, 6.0).astype(jnp.bfloat16)


def place_ends(result, stream_key, least, high):
    shape = result.shape
    place = [jax.random.randint(jax.random.fold_in(stream_key, axis), (), 0, shape[axis]) for axis in range(len(shape))]
    result = result.at[tuple(place)].set(least)
    longest = shape.index(max(shape))
    place[longest] = (place[longest] + 1) % shape[longest]
    return result.at[tuple(place)].set(high)


def levels(stream_key, extent, pieces, low, largest):
    loudness = 1.0
    for dim, parts in pieces:
        heights = jax.random.uniform(jax.random.fold_in(jax.random.fold_in(stream_key, 6), dim), (parts,), jnp.float32, low / len(pieces), largest / len(pieces))
        loudness = loudness * jnp.repeat(jnp.exp(heights), extent[dim] // parts).reshape((-1,) + (1,) * (len(extent) - 1 - dim))
    return loudness


def bell_draw(rng, extent, scale, reach, cuts=(), held_as=jnp.bfloat16):
    entries = scale * jax.random.normal(rng, extent, jnp.float32)
    if cuts:
        entries = entries * levels(rng, extent, cuts, -0.22, 0.18)
    return jnp.clip(entries, -reach, reach).astype(held_as)


def setup_inputs(seed: int = 0) -> dict:
    keys = jax.random.split(jax.random.key(seed), 8)
    noise = draw_noise(jax.random.fold_in(keys[7], 71), 0)
    data = draw_data(jax.random.fold_in(keys[7], 71), 0)
    t_index = place_ends(jax.random.randint(keys[2], (BATCH,), 0, TGRID + 1), jax.random.fold_in(keys[2], 1), 0, TGRID).astype(jnp.int32)
    embed_weight = bell_draw(keys[3], (PATCH_IN, WIDTH), PATCH_IN ** -0.5, 0.75)
    position = bell_draw(keys[4], (NPATCH, WIDTH), 1.0, 6.0)
    norm_gain = jnp.clip(1.0 + 0.1 * jax.random.normal(keys[5], (WIDTH,), jnp.float32), 0.5, 1.5)
    qkv_weight = bell_draw(keys[6], (WIDTH, QKV), WIDTH ** -0.5, 0.125, ((1, 16),))
    return {"noise": noise, "data": data, "t_index": t_index, "embed_weight": embed_weight, "position": position, "norm_gain": norm_gain, "qkv_weight": qkv_weight}


def reference(noise, data, t_index, embed_weight, position, norm_gain, qkv_weight):
    noise_f = noise.astype(jnp.float32)
    data_f = data.astype(jnp.float32)
    noise_sq = lax.optimization_barrier(jnp.sum(noise_f * noise_f, axis=1))
    data_sq = lax.optimization_barrier(jnp.sum(data_f * data_f, axis=1))
    cross_term = jnp.dot(noise, data.T, preferred_element_type=jnp.float32)
    cost = (noise_sq[:, None] + data_sq[None, :] - 2.0 * cross_term) / LATENT
    col_pot = jnp.zeros((BATCH,), jnp.float32)
    epsilon = 0.04
    for step in range(ITERS):
        epsilon = 0.04 * 0.45 ** step
        row_pot = -epsilon * jax.nn.logsumexp((col_pot[None, :] - cost) / epsilon, axis=1)
        col_pot = -epsilon * jax.nn.logsumexp((row_pot[:, None] - cost) / epsilon, axis=0)
    scores = (col_pot[None, :] - cost) / epsilon
    peak = lax.optimization_barrier(jnp.max(scores, axis=1, keepdims=True))
    expo = jnp.exp(scores - peak)
    denom = lax.optimization_barrier(jnp.sum(expo, axis=1))
    coupling = expo.astype(jnp.bfloat16)
    target = jnp.dot(coupling, data, preferred_element_type=jnp.float32) / denom[:, None]
    velocity = (target - noise_f).astype(jnp.bfloat16)
    times = t_index.astype(jnp.float32) / TGRID
    mixed = ((1.0 - times)[:, None] * noise_f + times[:, None] * target).astype(jnp.bfloat16)
    patches = mixed.reshape(BATCH * NPATCH, PATCH_IN)
    embedded = jnp.dot(patches, embed_weight, preferred_element_type=jnp.float32).reshape(BATCH, NPATCH, WIDTH)
    embedded = embedded + position.astype(jnp.float32)[None]
    meansq = lax.optimization_barrier(jnp.mean(embedded * embedded, axis=-1, keepdims=True))
    normed = (embedded * jax.lax.rsqrt(meansq + 1e-06) * norm_gain).astype(jnp.bfloat16).reshape(BATCH * NPATCH, WIDTH)
    qkv = jnp.dot(normed, qkv_weight, preferred_element_type=jnp.float32).astype(jnp.bfloat16)
    return (velocity, qkv)
```

```python
import jax
import jax.numpy as jnp
from jax import lax
from jax.sharding import PartitionSpec as P

ITERS = 3
TGRID = 1000


def shared(value, axis, count):
    spread = lax.optimization_barrier(jnp.broadcast_to(value[None], (count,) + value.shape))
    return lax.all_to_all(spread, axis, 0, 0)


def lse(scores, dim):
    peak = jnp.max(scores, axis=dim, keepdims=True)
    total = jnp.sum(jnp.exp(scores - peak), axis=dim)
    return jnp.squeeze(peak, dim) + jnp.log(total)


def halves(value):
    high = value.astype(jnp.bfloat16)
    low = (value - high.astype(jnp.float32)).astype(jnp.bfloat16)
    return high, low


def folded_weights(embed_weight, position, norm_gain, qkv_weight):
    scaled = jnp.concatenate([embed_weight, position], 0).astype(jnp.float32) * norm_gain
    high, low = halves(scaled)
    both = jnp.dot(
        jnp.concatenate([high, low], 0), qkv_weight, preferred_element_type=jnp.float32
    )
    rows = scaled.shape[0]
    return jnp.concatenate(halves(both[:rows] + both[rows:]), 0)


def local(noise, data, t_index, embed_weight, position, norm_gain, qkv_weight):
    latent = noise.shape[1]
    own = noise.shape[0]
    n_src = lax.axis_size("src")
    n_tgt = lax.axis_size("tgt")
    folded = lax.all_gather(
        folded_weights(embed_weight, position, norm_gain, qkv_weight), "tgt", axis=1, tiled=True
    )
    noise_block = lax.all_gather(noise, "tgt", axis=0, tiled=True)
    data_block = lax.all_gather(data, "src", axis=0, tiled=True)
    noise_sq = jnp.sum(jnp.square(noise_block.astype(jnp.float32)), axis=1)
    data_sq = jnp.sum(jnp.square(data_block.astype(jnp.float32)), axis=1)
    cross_term = lax.dot_general(
        noise_block, data_block, (((1,), (1,)), ((), ())), preferred_element_type=jnp.float32
    )
    cost = (noise_sq[:, None] + data_sq[None, :] - 2.0 * cross_term) / latent
    col_pot = jnp.zeros((data_block.shape[0],), jnp.float32)
    epsilon = 0.04
    for step in range(ITERS):
        epsilon = 0.04 * 0.45**step
        part = lse((col_pot[None, :] - cost) / epsilon, 1)
        row_pot = -epsilon * lse(shared(part, "tgt", n_tgt), 0)
        part = lse((row_pot[:, None] - cost) / epsilon, 0)
        col_pot = -epsilon * lse(shared(part, "src", n_src), 0)
    scores = (col_pot[None, :] - cost) / epsilon
    total = lse(shared(lse(scores, 1), "tgt", n_tgt), 0)
    coupling = jnp.exp(scores - total[:, None]).astype(jnp.bfloat16)
    partial_sum = jnp.dot(coupling, data_block, preferred_element_type=jnp.float32)
    pieces = lax.all_to_all(
        partial_sum.astype(jnp.bfloat16).reshape(n_tgt, own, latent), "tgt", 0, 0
    )
    target = jnp.sum(pieces.astype(jnp.float32), axis=0)
    noise_own = noise.astype(jnp.float32)
    velocity = (target - noise_own).astype(jnp.bfloat16)
    times = t_index.astype(jnp.float32) / TGRID
    mixed = ((1.0 - times)[:, None] * noise_own + times[:, None] * target).astype(jnp.bfloat16)

    patch_in, width = embed_weight.shape
    patch_count = position.shape[0]
    patches = mixed.reshape(own * patch_count, patch_in)
    embedded = jnp.dot(patches, embed_weight, preferred_element_type=jnp.float32)
    embedded = embedded.reshape(own, patch_count, width) + position.astype(jnp.float32)[None]
    scale = lax.rsqrt(jnp.mean(embedded * embedded, axis=-1) + 1e-06).reshape(own * patch_count)
    place = jnp.tile(jnp.eye(patch_count, dtype=jnp.bfloat16), (own, 1))
    tokens = jnp.concatenate([patches, place, patches, place], 1)
    qkv = jnp.dot(tokens, folded, preferred_element_type=jnp.float32) * scale[:, None]
    return (velocity, qkv.astype(jnp.bfloat16))


def solution(mesh):
    return jax.shard_map(
        local,
        mesh=mesh,
        in_specs=(
            P(("src", "tgt"), None),
            P(("src", "tgt"), None),
            P(("src", "tgt")),
            P(),
            P(),
            P(),
            P(None, "tgt"),
        ),
        out_specs=(P(("src", "tgt"), None), P(("src", "tgt"), None)),
        check_vma=False,
    )
```

```python
import functools

import jax
import jax.numpy as jnp
from jax import lax
from jax.experimental import pallas as pl
from jax.experimental.pallas import tpu as pltpu
from jax.sharding import PartitionSpec as P

ITERS = 3
TGRID = 1000
BOTH = ("src", "tgt")
CORE, ZPAIR, ZFAR = 1, 2, 16 + 2
Y_STEPS = (4, 8, 12)
X_STEPS = (32, 64, 96)
QUARTERS = (1, 2, 3)
BF, F32 = jnp.bfloat16, jnp.float32


def epsilon_of(step):
    return 0.04 * 0.45**step


def swap(value, mask):
    return lax.ppermute(value, BOTH, [(i, i ^ mask) for i in range(128)])


def column_groups():
    groups = {}
    for i in range(128):
        groups.setdefault((((i >> 4) ^ (i >> 1)) & 1, i & 1), []).append(i)
    return [groups[key] for key in sorted(groups)]


def vmem_call(kernel, out_shape, scratch=(), smem=0, inputs=0, flops=0, nbytes=0):
    return pl.pallas_call(
        kernel,
        out_shape=out_shape,
        in_specs=[pl.BlockSpec(memory_space=pltpu.SMEM)] * smem
        + [pl.BlockSpec(memory_space=pltpu.VMEM)] * inputs,
        out_specs=jax.tree.map(lambda _: pl.BlockSpec(memory_space=pltpu.VMEM), out_shape),
        scratch_shapes=list(scratch),
        compiler_params=pltpu.CompilerParams(vmem_limit_bytes=48 * 1024 * 1024),
        cost_estimate=pl.CostEstimate(flops=flops, bytes_accessed=nbytes, transcendentals=0),
    )


def shape(dims, dtype=F32):
    return jax.ShapeDtypeStruct(dims, dtype)


def eye(size):
    return lax.broadcasted_iota(jnp.int32, (size, size), 0) == lax.broadcasted_iota(
        jnp.int32, (size, size), 1
    )


def to_lanes(column):
    size = column.shape[0]
    wide = jnp.broadcast_to(column, (size, size))
    return jnp.sum(jnp.where(eye(size), wide, 0.0), axis=0, keepdims=True)


def to_rows(lanes):
    size = lanes.shape[1]
    wide = jnp.broadcast_to(lanes, (size, size))
    return jnp.sum(jnp.where(eye(size), wide, 0.0), axis=1, keepdims=True)


def join_lse(parts):
    peak = functools.reduce(jnp.maximum, parts)
    total = functools.reduce(jnp.add, [jnp.exp(part - peak) for part in parts])
    return peak + jnp.log(total)


def row_stats(cost_ref, col_pot, inverse):
    tiles = cost_ref.shape[1] // 128

    def score(tile):
        part = cost_ref[:, tile * 128 : (tile + 1) * 128]
        if col_pot is None:
            return -part * inverse
        return (col_pot[tile : tile + 1, :] - part) * inverse

    peak = score(0)
    for tile in range(1, tiles):
        peak = jnp.maximum(peak, score(tile))
    peak = jnp.max(peak, axis=1, keepdims=True)
    return score, peak


def row_lse(cost_ref, col_pot, inverse):
    score, peak = row_stats(cost_ref, col_pot, inverse)
    total = jnp.exp(score(0) - peak)
    for tile in range(1, cost_ref.shape[1] // 128):
        total = total + jnp.exp(score(tile) - peak)
    return peak + jnp.log(jnp.sum(total, axis=1, keepdims=True))


def cost_kernel(place, n0, n1, n23, *refs):
    left, right = refs[:4], refs[4:8]
    data_ref, cost_ref, lse_ref, noise_ref = refs[8:]
    x, z, y, q = place[0], place[1], place[2], place[3]
    half = left[0].shape[-1]
    rows = n0.shape[0]
    noise_ref[q] = n0[...]
    noise_ref[q ^ 1] = n1[...]
    noise_ref[q ^ 2] = n23[0]
    noise_ref[q ^ 3] = n23[1]
    for a in range(4):
        for b in range(4):
            for c in range(2):
                slot = ((x ^ b) * 2 + (z ^ c)) * 4 + (y ^ a)
                data_ref[slot, :, 0:half] = left[a][b, c]
                slot = ((x ^ a) * 2 + (z ^ c)) * 4 + (y ^ b)
                data_ref[slot, :, half : 2 * half] = right[a][b, c]
    latent = 2 * half
    noise = noise_ref[...].reshape(4 * rows, latent)

    def square_sum(value):
        total = jnp.zeros((value.shape[0], 128), F32)
        for tile in range(latent // 128):
            part = value[:, tile * 128 : (tile + 1) * 128].astype(F32)
            total = total + part * part
        return jnp.sum(total, axis=1, keepdims=True)

    noise_sq = square_sum(noise)
    for group in range(4):
        part = data_ref[group * 8 : group * 8 + 8].reshape(8 * rows, latent)
        cross = lax.dot_general(
            noise, part, (((1,), (1,)), ((), ())), preferred_element_type=F32
        )
        for side in range(2):
            data_sq = to_lanes(square_sum(part[side * 128 : side * 128 + 128]))
            at = group * 256 + side * 128
            cost_ref[:, at : at + 128] = (
                noise_sq + data_sq - 2.0 * cross[:, side * 128 : side * 128 + 128]
            ) / latent
    lse = row_lse(cost_ref, None, 1.0 / epsilon_of(0))
    lse_ref[...] = jnp.broadcast_to(to_lanes(lse), lse_ref.shape)


def col_kernel(step, cost_ref, a, b, c, d, out_ref):
    epsilon = epsilon_of(step)
    joined = join_lse([a[...], b[...], c[...], d[...]])
    row_pot = to_rows(-epsilon * joined[0:1, :])
    scores = (row_pot - cost_ref[...]) * (1.0 / epsilon)
    peak = jnp.max(scores, axis=0, keepdims=True)
    lse = peak + jnp.log(jnp.sum(jnp.exp(scores - peak), axis=0, keepdims=True))
    place = lax.broadcasted_iota(jnp.int32, (8, 128), 0)
    packed = jnp.zeros((8, 128), F32)
    for tile in range(8):
        packed = jnp.where(place == tile, lse[:, tile * 128 : (tile + 1) * 128], packed)
    out_ref[...] = jnp.broadcast_to(packed[None], out_ref.shape)


def col_potential(step, parts_ref):
    parts = parts_ref[...]
    peak = jnp.max(parts, axis=0)
    total = jnp.sum(jnp.exp(parts - peak[None]), axis=0)
    return -epsilon_of(step) * (peak + jnp.log(total))


def row_kernel(step, cost_ref, parts_ref, lse_ref):
    lse = row_lse(cost_ref, col_potential(step - 1, parts_ref), 1.0 / epsilon_of(step))
    lse_ref[...] = jnp.broadcast_to(to_lanes(lse), lse_ref.shape)


def target_kernel(place, cost_ref, data_ref, parts_ref, own_ref, own_lse_ref, s1, s2, s3, coupling, sums, lses):
    q = place[3]
    col_pot = col_potential(ITERS - 1, parts_ref)
    score, peak = row_stats(cost_ref, col_pot, 1.0 / epsilon_of(ITERS - 1))
    total = jnp.zeros(cost_ref.shape[:1] + (128,), F32)
    for tile in range(8):
        expo = jnp.exp(score(tile) - peak)
        total = total + expo
        coupling[:, tile * 128 : (tile + 1) * 128] = expo.astype(BF)
    denom = jnp.sum(total, axis=1, keepdims=True)
    rows = sums.shape[1]
    lses[...] = jnp.broadcast_to(peak + jnp.log(denom), (4 * rows, 128)).reshape(4, rows, 128)
    latent = sums.shape[2]
    for at in range(0, latent, 512):
        part = data_ref[:, :, at : at + 512].reshape(-1, 512)
        product = jnp.dot(coupling[...], part, preferred_element_type=F32) / denom
        sums[:, :, at : at + 512] = product.reshape(4, rows, 512)
    own_ref[...] = sums[q]
    own_lse_ref[...] = lses[q]
    lane = lax.broadcasted_iota(jnp.int32, (rows, 128), 1)
    for mask, out in ((1, s1), (2, s2), (3, s3)):
        out[:, 0:latent] = sums[q ^ mask].astype(BF)
        value = lses[q ^ mask]
        high = value.astype(BF).astype(F32)
        middle = (value - high).astype(BF).astype(F32)
        low = value - high - middle
        out[:, latent : latent + 128] = jnp.where(
            lane == 0, high, jnp.where(lane == 1, middle, jnp.where(lane == 2, low, 0.0))
        ).astype(BF)


def halves(value):
    high = value.astype(BF)
    low = (value - high.astype(F32)).astype(BF)
    return high, low


def folded_weights(embed_weight, position, norm_gain, qkv_weight):
    scaled = jnp.concatenate([embed_weight, position], 0).astype(F32) * norm_gain
    high, low = halves(scaled)
    both = jnp.dot(jnp.concatenate([high, low], 0), qkv_weight, preferred_element_type=F32)
    rows = scaled.shape[0]
    return jnp.concatenate(halves(both[:rows] + both[rows:]), 0)


def coupled_target(noise, data, place):
    rows, latent = noise.shape
    half = latent // 2
    far = swap(data, ZFAR)
    noise_core = swap(noise, CORE)
    first = [jnp.stack([data[:, s], far[:, s]]) for s in (slice(0, half), slice(half, latent))]
    noise_pair = swap(jnp.stack([noise, noise_core]), ZPAIR)
    left = jnp.stack([first[0]] + [swap(first[0], mask) for mask in X_STEPS])
    right = jnp.stack([first[1]] + [swap(first[1], mask) for mask in Y_STEPS])
    lefts = [left] + [swap(left, mask) for mask in Y_STEPS]
    rights = [right] + [swap(right, mask) for mask in X_STEPS]
    data_all, cost, row_part = vmem_call(
        cost_kernel,
        (shape((32, rows, latent), BF), shape((4 * rows, 32 * rows)), shape((8, 128))),
        scratch=[pltpu.VMEM((4, rows, latent), BF)],
        smem=1,
        inputs=11,
        flops=2 * 4 * rows * 32 * rows * latent,
        nbytes=8 * 1024 * 1024,
    )(place, noise, noise_core, noise_pair, *lefts, *rights)
    groups = column_groups()
    for step in range(ITERS):
        parts = [row_part] + [swap(row_part, mask) for mask in QUARTERS]
        col_part = vmem_call(
            functools.partial(col_kernel, step), shape((32, 8, 128)), inputs=5, nbytes=1024 * 1024
        )(cost, *parts)
        col_parts = lax.all_to_all(
            col_part, BOTH, 0, 0, axis_index_groups=groups, tiled=True
        )
        if step + 1 < ITERS:
            row_part = vmem_call(
                functools.partial(row_kernel, step + 1),
                shape((8, 128)),
                inputs=2,
                nbytes=1024 * 1024,
            )(cost, col_parts)
    own, own_lse, *sends = vmem_call(
        target_kernel,
        (shape((rows, latent)), shape((rows, 128))) + (shape((rows, latent + 128), BF),) * 3,
        scratch=[
            pltpu.VMEM((4 * rows, 32 * rows), BF),
            pltpu.VMEM((4, rows, latent), F32),
            pltpu.VMEM((4, rows, 128), F32),
        ],
        smem=1,
        inputs=3,
        flops=2 * 4 * rows * 32 * rows * latent,
        nbytes=6 * 1024 * 1024,
    )(place, cost, data_all, col_parts)
    others = [swap(send, mask) for send, mask in zip(sends, QUARTERS)]
    logs = [own_lse[:, 0]] + [
        jnp.sum(other[:, latent : latent + 3].astype(F32), axis=1) for other in others
    ]
    total = join_lse(logs)
    target = own * jnp.exp(logs[0] - total)[:, None]
    for other, log in zip(others, logs[1:]):
        target = target + other[:, :latent].astype(F32) * jnp.exp(log - total)[:, None]
    return target


def local(noise, data, t_index, embed_weight, position, norm_gain, qkv_weight):
    own = noise.shape[0]
    src, tgt = lax.axis_index("src"), lax.axis_index("tgt")
    place = jnp.stack([src // 2, src % 2, tgt // 4, tgt % 4]).astype(jnp.int32)
    folded = lax.all_gather(
        folded_weights(embed_weight, position, norm_gain, qkv_weight), "tgt", axis=1, tiled=True
    )
    target = coupled_target(noise, data, place)
    noise_own = noise.astype(F32)
    velocity = (target - noise_own).astype(BF)
    times = t_index.astype(F32) / TGRID
    mixed = ((1.0 - times)[:, None] * noise_own + times[:, None] * target).astype(BF)

    patch_in, width = embed_weight.shape
    patch_count = position.shape[0]
    patches = mixed.reshape(own * patch_count, patch_in)
    embedded = jnp.dot(patches, embed_weight, preferred_element_type=F32)
    embedded = embedded.reshape(own, patch_count, width) + position.astype(F32)[None]
    scale = lax.rsqrt(jnp.mean(embedded * embedded, axis=-1) + 1e-06).reshape(own * patch_count)
    spots = jnp.tile(jnp.eye(patch_count, dtype=BF), (own, 1))
    tokens = jnp.concatenate([patches, spots, patches, spots], 1)
    qkv = jnp.dot(tokens, folded, preferred_element_type=F32) * scale[:, None]
    return (velocity, qkv.astype(BF))


def solution(mesh):
    return jax.shard_map(
        local,
        mesh=mesh,
        in_specs=(
            P(("src", "tgt"), None),
            P(("src", "tgt"), None),
            P(("src", "tgt")),
            P(),
            P(),
            P(),
            P(None, "tgt"),
        ),
        out_specs=(P(("src", "tgt"), None), P(("src", "tgt"), None)),
        check_vma=False,
    )
```

```python
import functools

import jax
import jax.numpy as jnp
from jax import lax
from jax.experimental import pallas as pl
from jax.experimental.pallas import tpu as pltpu
from jax.sharding import PartitionSpec as P

ITERS = 3
TGRID = 1000
BOTH = ("src", "tgt")
CORE = 1
Z_STEPS = (2, 16, 18)
Y_STEPS = (4, 8, 12)
X_STEPS = (32, 64, 96)
BF, F32 = jnp.bfloat16, jnp.float32


def epsilon_of(step):
    return 0.04 * 0.45**step


def swap(value, mask):
    return lax.ppermute(value, BOTH, [(i, i ^ mask) for i in range(128)])


def column_groups():
    groups = {}
    for i in range(128):
        groups.setdefault(((i >> 4) & 1, i & 3), []).append(i)
    return [groups[key] for key in sorted(groups)]


def vmem_call(kernel, out_shape, scratch=(), smem=0, inputs=0, flops=0, nbytes=0):
    return pl.pallas_call(
        kernel,
        out_shape=out_shape,
        in_specs=[pl.BlockSpec(memory_space=pltpu.SMEM)] * smem
        + [pl.BlockSpec(memory_space=pltpu.VMEM)] * inputs,
        out_specs=jax.tree.map(lambda _: pl.BlockSpec(memory_space=pltpu.VMEM), out_shape),
        scratch_shapes=list(scratch),
        compiler_params=pltpu.CompilerParams(vmem_limit_bytes=48 * 1024 * 1024),
        cost_estimate=pl.CostEstimate(flops=flops, bytes_accessed=nbytes, transcendentals=0),
    )


def shape(dims, dtype=F32):
    return jax.ShapeDtypeStruct(dims, dtype)


def eye(size):
    return lax.broadcasted_iota(jnp.int32, (size, size), 0) == lax.broadcasted_iota(
        jnp.int32, (size, size), 1
    )


def to_lanes(column):
    size = column.shape[0]
    wide = jnp.broadcast_to(column, (size, size))
    return jnp.sum(jnp.where(eye(size), wide, 0.0), axis=0, keepdims=True)


def to_rows(lanes):
    size = lanes.shape[1]
    wide = jnp.broadcast_to(lanes, (size, size))
    return jnp.sum(jnp.where(eye(size), wide, 0.0), axis=1, keepdims=True)


def join_lse(parts):
    peak = functools.reduce(jnp.maximum, parts)
    total = functools.reduce(jnp.add, [jnp.exp(part - peak) for part in parts])
    return peak + jnp.log(total)


def row_stats(cost_ref, col_pot, inverse):
    tiles = cost_ref.shape[1] // 128

    def score(tile):
        part = cost_ref[:, tile * 128 : (tile + 1) * 128]
        if col_pot is None:
            return -part * inverse
        return (col_pot[tile : tile + 1, :] - part) * inverse

    peak = score(0)
    for tile in range(1, tiles):
        peak = jnp.maximum(peak, score(tile))
    peak = jnp.max(peak, axis=1, keepdims=True)
    return score, peak


def row_lse(cost_ref, col_pot, inverse):
    score, peak = row_stats(cost_ref, col_pot, inverse)
    total = jnp.exp(score(0) - peak)
    for tile in range(1, cost_ref.shape[1] // 128):
        total = total + jnp.exp(score(tile) - peak)
    return peak + jnp.log(jnp.sum(total, axis=1, keepdims=True))


def pack(lse, out_ref):
    out_ref[...] = jnp.zeros(out_ref.shape, F32)
    for part in range(lse.shape[0] // 128):
        out_ref[part : part + 1, :] = to_lanes(lse[part * 128 : part * 128 + 128])


def cost_kernel(place, data_ref, a, b, c, d, cost_ref, lse_ref, noise_ref):
    h = place[2]
    rows, latent = a.shape[1:]
    for k, pair in enumerate((a, b, c, d)):
        noise_ref[h ^ (2 * k)] = pair[0]
        noise_ref[h ^ (2 * k + 1)] = pair[1]
    noise = noise_ref[...].reshape(8 * rows, latent)

    def square_sum(value):
        total = jnp.zeros((value.shape[0], 128), F32)
        for tile in range(latent // 128):
            part = value[:, tile * 128 : (tile + 1) * 128].astype(F32)
            total = total + part * part
        return jnp.sum(total, axis=1, keepdims=True)

    noise_sq = square_sum(noise)
    for group in range(2):
        part = data_ref[group * 8 : group * 8 + 8].reshape(8 * rows, latent)
        cross = lax.dot_general(
            noise, part, (((1,), (1,)), ((), ())), preferred_element_type=F32
        )
        for side in range(2):
            data_sq = to_lanes(square_sum(part[side * 128 : side * 128 + 128]))
            at = group * 256 + side * 128
            cost_ref[:, at : at + 128] = (
                noise_sq + data_sq - 2.0 * cross[:, side * 128 : side * 128 + 128]
            ) / latent
    pack(row_lse(cost_ref, None, 1.0 / epsilon_of(0)), lse_ref)


def col_kernel(step, cost_ref, a, b, c, d, out_ref):
    epsilon = epsilon_of(step)
    joined = -epsilon * join_lse([a[...], b[...], c[...], d[...]])
    halfway = cost_ref.shape[0] // 2
    inverse = 1.0 / epsilon
    upper = (to_rows(joined[0:1, :]) - cost_ref[0:halfway, :]) * inverse
    lower = (to_rows(joined[1:2, :]) - cost_ref[halfway : 2 * halfway, :]) * inverse
    peak = jnp.maximum(
        jnp.max(upper, axis=0, keepdims=True), jnp.max(lower, axis=0, keepdims=True)
    )
    total = jnp.sum(jnp.exp(upper - peak) + jnp.exp(lower - peak), axis=0, keepdims=True)
    lse = peak + jnp.log(total)
    place = lax.broadcasted_iota(jnp.int32, (8, 128), 0)
    packed = jnp.zeros((8, 128), F32)
    for tile in range(lse.shape[1] // 128):
        packed = jnp.where(place == tile, lse[:, tile * 128 : (tile + 1) * 128], packed)
    out_ref[...] = jnp.broadcast_to(packed[None], out_ref.shape)


def col_potential(step, parts_ref):
    parts = parts_ref[...]
    peak = jnp.max(parts, axis=0)
    total = jnp.sum(jnp.exp(parts - peak[None]), axis=0)
    return -epsilon_of(step) * (peak + jnp.log(total))


def row_kernel(step, cost_ref, parts_ref, lse_ref):
    pack(row_lse(cost_ref, col_potential(step - 1, parts_ref), 1.0 / epsilon_of(step)), lse_ref)


def packed_log(value):
    lane = lax.broadcasted_iota(jnp.int32, value.shape, 1)
    high = value.astype(BF).astype(F32)
    middle = (value - high).astype(BF).astype(F32)
    low = value - high - middle
    return jnp.where(
        lane == 0, high, jnp.where(lane == 1, middle, jnp.where(lane == 2, low, 0.0))
    ).astype(BF)


def target_kernel(place, cost_ref, data_ref, parts_ref, keep_ref, log_ref, send_ref, coupling, sums, lses):
    h = place[2]
    col_pot = col_potential(ITERS - 1, parts_ref)
    score, peak = row_stats(cost_ref, col_pot, 1.0 / epsilon_of(ITERS - 1))
    total = jnp.zeros(cost_ref.shape[:1] + (128,), F32)
    for tile in range(cost_ref.shape[1] // 128):
        expo = jnp.exp(score(tile) - peak)
        total = total + expo
        coupling[:, tile * 128 : (tile + 1) * 128] = expo.astype(BF)
    denom = jnp.sum(total, axis=1, keepdims=True)
    count, rows, latent = sums.shape
    lses[...] = jnp.broadcast_to(peak + jnp.log(denom), (count * rows, 128)).reshape(lses.shape)
    share = 1.0 / denom
    for at in range(0, latent, 512):
        part = data_ref[:, :, at : at + 512].reshape(-1, 512)
        product = jnp.dot(coupling[...], part, preferred_element_type=F32) * share
        sums[:, :, at : at + 512] = product.reshape(count, rows, 512)
    for k in range(4):
        keep_ref[k] = sums[h ^ (2 * k)]
        log_ref[k] = lses[h ^ (2 * k)]
        send_ref[k, :, 0:latent] = sums[h ^ (2 * k + 1)].astype(BF)
        send_ref[k, :, latent : latent + 128] = packed_log(lses[h ^ (2 * k + 1)])


def read_log(ref_value):
    return jnp.sum(ref_value.astype(F32), axis=1, keepdims=True)


def pair_kernel(keep_ref, log_ref, got_ref, own_ref, own_log_ref, s1, s2, s3):
    latent = keep_ref.shape[2]
    for k, out in enumerate((own_ref, s1, s2, s3)):
        first = log_ref[k]
        second = jnp.broadcast_to(read_log(got_ref[k, :, latent : latent + 128]), first.shape)
        total = join_lse([first, second])
        mixed = keep_ref[k] * jnp.exp(first - total)[:, 0:1] + got_ref[
            k, :, 0:latent
        ].astype(F32) * jnp.exp(second - total)[:, 0:1]
        if k == 0:
            out[...] = mixed
            own_log_ref[...] = total
        else:
            out[:, 0:latent] = mixed.astype(BF)
            out[:, latent : latent + 128] = packed_log(total)


def finish_kernel(own_ref, log_ref, a, b, c, noise_ref, time_ref, velocity_ref, mixed_ref):
    latent = own_ref.shape[1]
    logs = [log_ref[...]] + [
        jnp.broadcast_to(read_log(got[:, latent : latent + 128]), log_ref.shape)
        for got in (a, b, c)
    ]
    total = join_lse(logs)
    shares = [jnp.exp(log - total)[:, 0:1] for log in logs]
    times = time_ref[...].astype(F32) / TGRID
    for at in range(0, latent, 256):
        cut = slice(at, at + 256)
        target = own_ref[:, cut] * shares[0]
        for got, share in zip((a, b, c), shares[1:]):
            target = target + got[:, cut].astype(F32) * share
        noise = noise_ref[:, cut].astype(F32)
        velocity_ref[:, cut] = (target - noise).astype(BF)
        mixed_ref[:, cut] = ((1.0 - times) * noise + times * target).astype(BF)


def qkv_kernel(place, tokens_ref, table_ref, f0, f1, f2, f3, out_ref):
    width = table_ref.shape[1]
    chunk = tokens_ref[...]
    count = chunk.shape[0]
    total = jnp.zeros((count, 128), F32)
    for col in range(0, width, 256):
        part = jnp.dot(chunk, table_ref[:, col : col + 256], preferred_element_type=F32)
        part = part * part
        total = total + part[:, 0:128] + part[:, 128:256]
    scale = lax.rsqrt(jnp.sum(total, axis=1, keepdims=True) / width + 1e-06)
    columns = f0.shape[2]
    for k in range(16):
        folded = (f0, f1, f2, f3)[k // 4][k % 4]
        product = jnp.dot(chunk, folded, preferred_element_type=F32) * scale
        at = pl.multiple_of((place[3] ^ k) * columns, 128)
        out_ref[:, pl.ds(at, columns)] = product.astype(BF)


def halves(value):
    high = value.astype(BF)
    low = (value - high.astype(F32)).astype(BF)
    return high, low


def folded_weights(embed_weight, position, norm_gain, qkv_weight):
    scaled = jnp.concatenate([embed_weight, position], 0).astype(F32) * norm_gain
    high, low = halves(scaled)
    both = jnp.dot(jnp.concatenate([high, low], 0), qkv_weight, preferred_element_type=F32)
    rows = scaled.shape[0]
    return jnp.concatenate(halves(both[:rows] + both[rows:]), 0)


def together(*values):
    return lax.optimization_barrier(values)


def coupled_target(noise, data, t_index, place, folded):
    rows, latent = noise.shape
    groups = column_groups()
    noise_pair = jnp.stack([noise, swap(noise, CORE)])
    noises = [noise_pair] + [swap(noise_pair, mask) for mask in Z_STEPS]
    spread = jnp.broadcast_to(data[None], (16, rows, latent)).reshape(16 * rows, latent)
    data_all = lax.all_to_all(
        lax.optimization_barrier(spread), BOTH, 0, 0, axis_index_groups=groups, tiled=True
    ).reshape(16, rows, latent)
    flops = 2 * 8 * rows * 16 * rows * latent
    cost, row_part = vmem_call(
        cost_kernel,
        (shape((8 * rows, 16 * rows)), shape((8, 128))),
        scratch=[pltpu.VMEM((8, rows, latent), BF)],
        smem=1,
        inputs=5,
        flops=flops,
        nbytes=4 * 1024 * 1024,
    )(place, data_all, *noises)
    quads = [None] * 4
    folded, row_part = together(folded, row_part)
    folded = jnp.stack([folded, swap(folded, CORE)])
    for step in range(ITERS):
        if step == 1:
            folded, row_part = together(folded, row_part)
            quads = [folded, swap(folded, Y_STEPS[0]), None, swap(folded, Y_STEPS[2])]
        elif step == 2:
            folded, row_part = together(folded, row_part)
            quads[2] = swap(folded, Y_STEPS[1])
        row_pair = join_lse([row_part, swap(row_part, CORE)])
        parts = [row_pair] + [swap(row_pair, mask) for mask in Z_STEPS]
        col_part = vmem_call(
            functools.partial(col_kernel, step), shape((16, 8, 128)), inputs=5, nbytes=1024 * 1024
        )(cost, *parts)
        if step == 0:
            folded, col_part = together(folded, col_part)
            folded = jnp.concatenate([folded, swap(folded, Z_STEPS[0])])
        col_parts = lax.all_to_all(
            col_part, BOTH, 0, 0, axis_index_groups=groups, tiled=True
        )
        if step == 0:
            folded, col_parts = together(folded, col_parts)
        elif step == 1:
            quads[1], quads[3], col_parts = together(quads[1], quads[3], col_parts)
        elif step == 2:
            quads[2], col_parts = together(quads[2], col_parts)
        if step + 1 < ITERS:
            row_part = vmem_call(
                functools.partial(row_kernel, step + 1),
                shape((8, 128)),
                inputs=2,
                nbytes=1024 * 1024,
            )(cost, col_parts)
    keep, log, send = vmem_call(
        target_kernel,
        (
            shape((4, rows, latent)),
            shape((4, rows, 128)),
            shape((4, rows, latent + 128), BF),
        ),
        scratch=[
            pltpu.VMEM((8 * rows, 16 * rows), BF),
            pltpu.VMEM((8, rows, latent), F32),
            pltpu.VMEM((8, rows, 128), F32),
        ],
        smem=1,
        inputs=3,
        flops=flops,
        nbytes=6 * 1024 * 1024,
    )(place, cost, data_all, col_parts)
    own, own_log, *sends = vmem_call(
        pair_kernel,
        (shape((rows, latent)), shape((rows, 128))) + (shape((rows, latent + 128), BF),) * 3,
        inputs=3,
        nbytes=2 * 1024 * 1024,
    )(keep, log, swap(send, CORE))
    others = [swap(value, mask) for value, mask in zip(sends, Z_STEPS)]
    velocity, mixed = vmem_call(
        finish_kernel, (shape((rows, latent), BF),) * 2, inputs=7, nbytes=1024 * 1024
    )(own, own_log, *others, noise, t_index[:, None])
    return velocity, mixed, quads


def local(noise, data, t_index, embed_weight, position, norm_gain, qkv_weight):
    own = noise.shape[0]
    src, tgt = lax.axis_index("src"), lax.axis_index("tgt")
    ring = (src % 2) * 4 + tgt % 4
    place = jnp.stack([src // 2, tgt // 4, ring, tgt]).astype(jnp.int32)
    folded = folded_weights(embed_weight, position, norm_gain, qkv_weight)
    velocity, mixed, quads = coupled_target(noise, data, t_index, place, folded)
    patch_in, width = embed_weight.shape
    patch_count = position.shape[0]
    patches = mixed.reshape(own * patch_count, patch_in)
    spots = jnp.tile(jnp.eye(patch_count, dtype=BF), (own, 1))
    tokens = jnp.concatenate([patches, spots, patches, spots], 1)
    table = jnp.concatenate([embed_weight, position], 0)
    table = jnp.concatenate([table, jnp.zeros_like(table)], 0)
    quad, depth, columns = quads[0].shape
    count = 4 * quad
    chunk = 256
    whole = pl.BlockSpec((quad, depth, columns), lambda j, where: (0, 0, 0))
    qkv = pl.pallas_call(
        qkv_kernel,
        out_shape=shape((own * patch_count, count * columns), BF),
        grid_spec=pltpu.PrefetchScalarGridSpec(
            num_scalar_prefetch=1,
            grid=(own * patch_count // chunk,),
            in_specs=[
                pl.BlockSpec((chunk, depth), lambda j, where: (j, 0)),
                pl.BlockSpec((depth, width), lambda j, where: (0, 0)),
            ]
            + [whole] * 4,
            out_specs=pl.BlockSpec((chunk, count * columns), lambda j, where: (j, 0)),
        ),
        compiler_params=pltpu.CompilerParams(vmem_limit_bytes=48 * 1024 * 1024),
        cost_estimate=pl.CostEstimate(
            flops=2 * own * patch_count * depth * count * columns,
            bytes_accessed=16 * 1024 * 1024,
            transcendentals=0,
        ),
    )(place, tokens, table, *quads)
    return (velocity, qkv)


def solution(mesh):
    return jax.shard_map(
        local,
        mesh=mesh,
        in_specs=(
            P(("src", "tgt"), None),
            P(("src", "tgt"), None),
            P(("src", "tgt")),
            P(),
            P(),
            P(),
            P(None, "tgt"),
        ),
        out_specs=(P(("src", "tgt"), None), P(("src", "tgt"), None)),
        check_vma=False,
    )
```

```python
import functools

import jax
import jax.numpy as jnp
from jax import lax
from jax.experimental import pallas as pl
from jax.experimental.pallas import tpu as pltpu
from jax.sharding import PartitionSpec as P

ITERS = 3
TGRID = 1000
BOTH = ("src", "tgt")
CORE = 1
ROW_MASK, COL_MASK = 108, 19
Z_STEPS = (2, 16, 18)
Y_STEPS = (4, 8, 12)
X_STEPS = (32, 64, 96)
BF, F32 = jnp.bfloat16, jnp.float32


def epsilon_of(step):
    return 0.04 * 0.45**step


def swap(value, mask):
    return lax.ppermute(value, BOTH, [(i, i ^ mask) for i in range(128)])


def groups_by(mask):
    groups = {}
    for i in range(128):
        groups.setdefault(i & mask, []).append(i)
    return [groups[key] for key in sorted(groups)]


def exchange(value, mask):
    return lax.all_to_all(value, BOTH, 0, 0, axis_index_groups=groups_by(mask), tiled=True)


def vmem_call(kernel, out_shape, scratch=(), smem=0, inputs=0, flops=0, nbytes=0):
    return pl.pallas_call(
        kernel,
        out_shape=out_shape,
        in_specs=[pl.BlockSpec(memory_space=pltpu.SMEM)] * smem
        + [pl.BlockSpec(memory_space=pltpu.VMEM)] * inputs,
        out_specs=jax.tree.map(lambda _: pl.BlockSpec(memory_space=pltpu.VMEM), out_shape),
        scratch_shapes=list(scratch),
        compiler_params=pltpu.CompilerParams(vmem_limit_bytes=48 * 1024 * 1024),
        cost_estimate=pl.CostEstimate(flops=flops, bytes_accessed=nbytes, transcendentals=0),
    )


def shape(dims, dtype=F32):
    return jax.ShapeDtypeStruct(dims, dtype)


def eye(size):
    return lax.broadcasted_iota(jnp.int32, (size, size), 0) == lax.broadcasted_iota(
        jnp.int32, (size, size), 1
    )


def to_lanes(column):
    size = column.shape[0]
    wide = jnp.broadcast_to(column, (size, size))
    return jnp.sum(jnp.where(eye(size), wide, 0.0), axis=0, keepdims=True)


def to_rows(lanes):
    size = lanes.shape[1]
    wide = jnp.broadcast_to(lanes, (size, size))
    return jnp.sum(jnp.where(eye(size), wide, 0.0), axis=1, keepdims=True)


def join_lse(parts):
    peak = functools.reduce(jnp.maximum, parts)
    total = functools.reduce(jnp.add, [jnp.exp(part - peak) for part in parts])
    return peak + jnp.log(total)


def row_stats(cost_ref, col_pot, inverse):
    tiles = cost_ref.shape[1] // 128

    def score(tile):
        part = cost_ref[:, tile * 128 : (tile + 1) * 128]
        if col_pot is None:
            return -part * inverse
        return (col_pot[tile : tile + 1, :] - part) * inverse

    peak = score(0)
    for tile in range(1, tiles):
        peak = jnp.maximum(peak, score(tile))
    peak = jnp.max(peak, axis=1, keepdims=True)
    return score, peak


def row_lse(cost_ref, col_pot, inverse):
    score, peak = row_stats(cost_ref, col_pot, inverse)
    total = jnp.exp(score(0) - peak)
    for tile in range(1, cost_ref.shape[1] // 128):
        total = total + jnp.exp(score(tile) - peak)
    return peak + jnp.log(jnp.sum(total, axis=1, keepdims=True))


def pack(lse, out_ref):
    place = lax.broadcasted_iota(jnp.int32, (8, 128), 0)
    packed = jnp.zeros((8, 128), F32)
    for part in range(lse.shape[0] // 128):
        packed = jnp.where(place == part, to_lanes(lse[part * 128 : part * 128 + 128]), packed)
    out_ref[...] = jnp.broadcast_to(packed[None], out_ref.shape)


def spread_lse(parts):
    peak = jnp.max(parts, axis=0)
    return peak + jnp.log(jnp.sum(jnp.exp(parts - peak[None]), axis=0))


def cost_kernel(place, data_ref, a, b, c, d, cost_ref, lse_ref, noise_ref):
    h = place[2]
    rows, latent = a.shape[1:]
    for k, pair in enumerate((a, b, c, d)):
        noise_ref[h ^ (2 * k)] = pair[0]
        noise_ref[h ^ (2 * k + 1)] = pair[1]
    noise = noise_ref[...].reshape(8 * rows, latent)

    def square_sum(value):
        total = jnp.zeros((value.shape[0], 128), F32)
        for tile in range(latent // 128):
            part = value[:, tile * 128 : (tile + 1) * 128].astype(F32)
            total = total + part * part
        return jnp.sum(total, axis=1, keepdims=True)

    noise_sq = square_sum(noise)
    for group in range(2):
        part = data_ref[group * 8 : group * 8 + 8].reshape(8 * rows, latent)
        cross = lax.dot_general(
            noise, part, (((1,), (1,)), ((), ())), preferred_element_type=F32
        )
        for side in range(2):
            data_sq = to_lanes(square_sum(part[side * 128 : side * 128 + 128]))
            at = group * 256 + side * 128
            cost_ref[:, at : at + 128] = (
                noise_sq + data_sq - 2.0 * cross[:, side * 128 : side * 128 + 128]
            ) / latent
    pack(row_lse(cost_ref, None, 1.0 / epsilon_of(0)), lse_ref)


def col_kernel(step, cost_ref, parts_ref, out_ref):
    epsilon = epsilon_of(step)
    joined = -epsilon * spread_lse(parts_ref[...])
    halfway = cost_ref.shape[0] // 2
    inverse = 1.0 / epsilon
    upper = (to_rows(joined[0:1, :]) - cost_ref[0:halfway, :]) * inverse
    lower = (to_rows(joined[1:2, :]) - cost_ref[halfway : 2 * halfway, :]) * inverse
    peak = jnp.maximum(
        jnp.max(upper, axis=0, keepdims=True), jnp.max(lower, axis=0, keepdims=True)
    )
    total = jnp.sum(jnp.exp(upper - peak) + jnp.exp(lower - peak), axis=0, keepdims=True)
    lse = peak + jnp.log(total)
    place = lax.broadcasted_iota(jnp.int32, (8, 128), 0)
    packed = jnp.zeros((8, 128), F32)
    for tile in range(lse.shape[1] // 128):
        packed = jnp.where(place == tile, lse[:, tile * 128 : (tile + 1) * 128], packed)
    out_ref[...] = jnp.broadcast_to(packed[None], out_ref.shape)


def col_potential(step, parts_ref):
    return -epsilon_of(step) * spread_lse(parts_ref[...])


def row_kernel(step, cost_ref, parts_ref, lse_ref):
    pack(row_lse(cost_ref, col_potential(step - 1, parts_ref), 1.0 / epsilon_of(step)), lse_ref)


def packed_log(value):
    lane = lax.broadcasted_iota(jnp.int32, value.shape, 1)
    high = value.astype(BF).astype(F32)
    middle = (value - high).astype(BF).astype(F32)
    low = value - high - middle
    return jnp.where(
        lane == 0, high, jnp.where(lane == 1, middle, jnp.where(lane == 2, low, 0.0))
    ).astype(BF)


def target_kernel(place, cost_ref, data_ref, parts_ref, keep_ref, log_ref, send_ref, coupling, sums, lses):
    h = place[2]
    col_pot = col_potential(ITERS - 1, parts_ref)
    score, peak = row_stats(cost_ref, col_pot, 1.0 / epsilon_of(ITERS - 1))
    total = jnp.zeros(cost_ref.shape[:1] + (128,), F32)
    for tile in range(cost_ref.shape[1] // 128):
        expo = jnp.exp(score(tile) - peak)
        total = total + expo
        coupling[:, tile * 128 : (tile + 1) * 128] = expo.astype(BF)
    denom = jnp.sum(total, axis=1, keepdims=True)
    count, rows, latent = sums.shape
    lses[...] = jnp.broadcast_to(peak + jnp.log(denom), (count * rows, 128)).reshape(lses.shape)
    share = 1.0 / denom
    for at in range(0, latent, 512):
        part = data_ref[:, :, at : at + 512].reshape(-1, 512)
        product = jnp.dot(coupling[...], part, preferred_element_type=F32) * share
        sums[:, :, at : at + 512] = product.reshape(count, rows, 512)
    for k in range(4):
        keep_ref[k] = sums[h ^ (2 * k)]
        log_ref[k] = lses[h ^ (2 * k)]
        send_ref[k, :, 0:latent] = sums[h ^ (2 * k + 1)].astype(BF)
        send_ref[k, :, latent : latent + 128] = packed_log(lses[h ^ (2 * k + 1)])


def read_log(ref_value):
    return jnp.sum(ref_value.astype(F32), axis=1, keepdims=True)


def pair_kernel(keep_ref, log_ref, got_ref, own_ref, own_log_ref, s1, s2, s3):
    latent = keep_ref.shape[2]
    for k, out in enumerate((own_ref, s1, s2, s3)):
        first = log_ref[k]
        second = jnp.broadcast_to(read_log(got_ref[k, :, latent : latent + 128]), first.shape)
        total = join_lse([first, second])
        mixed = keep_ref[k] * jnp.exp(first - total)[:, 0:1] + got_ref[
            k, :, 0:latent
        ].astype(F32) * jnp.exp(second - total)[:, 0:1]
        if k == 0:
            out[...] = mixed
            own_log_ref[...] = total
        else:
            out[:, 0:latent] = mixed.astype(BF)
            out[:, latent : latent + 128] = packed_log(total)


def spread_kernel(value_ref, out_ref, sems):
    copies = [
        pltpu.make_async_copy(value_ref, out_ref.at[k], sems.at[k])
        for k in range(out_ref.shape[0])
    ]
    for copy in copies:
        copy.start()
    for copy in copies:
        copy.wait()


def qkv_kernel(
    place, own_ref, log_ref, noise_ref, time_ref, table_ref, *refs
):
    far = refs[:7]
    out_ref, velocity_ref, tokens = refs[7:10]
    near = refs[10:17]
    sems = refs[17]
    a, b, c, f0, f1, f2, f3 = near
    rows, latent = own_ref.shape
    step = pl.program_id(0)

    @pl.when(step == 0)
    def _():
        copies = [
            pltpu.make_async_copy(there, here, sems.at[k])
            for k, (there, here) in enumerate(zip(far, near))
        ]
        for copy in copies:
            copy.start()
        for copy in copies[:3]:
            copy.wait()
        logs = [log_ref[...]] + [
            jnp.broadcast_to(read_log(got[:, latent : latent + 128]), log_ref.shape)
            for got in (a, b, c)
        ]
        total = join_lse(logs)
        shares = [jnp.exp(log - total) for log in logs]
        times = jnp.broadcast_to(time_ref[...].astype(F32) / TGRID, (rows, 128))
        first = lax.broadcasted_iota(jnp.int32, (rows, 128), 1) < 64
        for tile in range(latent // 128):
            cut = slice(tile * 128, tile * 128 + 128)
            target = own_ref[:, cut] * shares[0]
            for got, share in zip((a, b, c), shares[1:]):
                target = target + got[:, cut].astype(F32) * share
            noise = noise_ref[:, cut].astype(F32)
            velocity_ref[:, cut] = (target - noise).astype(BF)
            mixed = ((1.0 - times) * noise + times * target).astype(BF).astype(F32)
            turned = pltpu.roll(mixed, 64, 1)
            tokens[pl.ds(2 * tile, rows, stride=latent // 64), :] = jnp.where(
                first, mixed, turned
            )
            tokens[pl.ds(2 * tile + 1, rows, stride=latent // 64), :] = jnp.where(
                first, turned, mixed
            )
        for copy in copies[3:]:
            copy.wait()

    count = out_ref.shape[0]
    width = table_ref.shape[1]
    patches = tokens[pl.ds(pl.multiple_of(step * count, count), count), :].astype(BF)
    spot = lax.broadcasted_iota(jnp.int32, (count, 128), 0) % 32
    lane = lax.broadcasted_iota(jnp.int32, (count, 128), 1)
    spots = jnp.where(spot == lane % 32, 1.0, 0.0).astype(BF)
    chunk = jnp.concatenate([patches, spots[:, 0:64]], axis=1)
    total = jnp.zeros((count, 128), F32)
    for col in range(0, width, 256):
        part = jnp.dot(chunk, table_ref[:, col : col + 256], preferred_element_type=F32)
        part = part * part
        total = total + part[:, 0:128] + part[:, 128:256]
    scale = lax.rsqrt(jnp.sum(total, axis=1, keepdims=True) / width + 1e-06)
    columns = f0.shape[1] // 4
    for k in range(0, 16, 2):
        at = (k % 4) * columns
        product = jnp.dot(
            chunk, (f0, f1, f2, f3)[k // 4][:, at : at + 2 * columns], preferred_element_type=F32
        )
        for side in range(2):
            to = pl.multiple_of((place[3] ^ (k + side)) * columns, 128)
            out_ref[:, pl.ds(to, columns)] = (
                product[:, side * columns : (side + 1) * columns] * scale
            ).astype(BF)


def halves(value):
    high = value.astype(BF)
    low = (value - high.astype(F32)).astype(BF)
    return high, low


def folded_weights(embed_weight, position, norm_gain, qkv_weight):
    scaled = jnp.concatenate([embed_weight, position], 0).astype(F32) * norm_gain
    high, low = halves(scaled)
    both = jnp.dot(jnp.concatenate([high, low], 0), qkv_weight, preferred_element_type=F32)
    rows = scaled.shape[0]
    high, low = halves(both[:rows] + both[rows:])
    split = embed_weight.shape[0]
    return jnp.concatenate([high[:split], low[:split], high[split:], low[split:]], 0)


def together(*values):
    return lax.optimization_barrier(values)


def coupled_target(noise, data, place, folded):
    rows, latent = noise.shape
    noise_pair = jnp.stack([noise, swap(noise, CORE)])
    noises = [noise_pair] + [swap(noise_pair, mask) for mask in Z_STEPS]
    spread = pl.pallas_call(
        spread_kernel,
        out_shape=shape((16, rows, latent), BF),
        in_specs=[pl.BlockSpec(memory_space=pltpu.VMEM)],
        out_specs=pl.BlockSpec(memory_space=pl.ANY),
        scratch_shapes=[pltpu.SemaphoreType.DMA((16,))],
    )(data)
    data_all = exchange(spread, COL_MASK)
    flops = 2 * 8 * rows * 16 * rows * latent
    cost, row_part = vmem_call(
        cost_kernel,
        (shape((8 * rows, 16 * rows)), shape((8, 8, 128))),
        scratch=[pltpu.VMEM((8, rows, latent), BF)],
        smem=1,
        inputs=5,
        flops=flops,
        nbytes=4 * 1024 * 1024,
    )(place, data_all, *noises)
    quads = [None] * 4
    folded, row_part = together(folded, row_part)
    folded = jnp.concatenate([folded, swap(folded, CORE)], 1)
    for step in range(ITERS):
        if step == 1:
            folded, row_part = together(folded, row_part)
            quads = [folded, swap(folded, Y_STEPS[0]), None, swap(folded, Y_STEPS[2])]
        elif step == 2:
            folded, row_part = together(folded, row_part)
            quads[2] = swap(folded, Y_STEPS[1])
        row_parts = exchange(row_part, ROW_MASK)
        col_part = vmem_call(
            functools.partial(col_kernel, step), shape((16, 8, 128)), inputs=2, nbytes=1024 * 1024
        )(cost, row_parts)
        if step == 0:
            folded, col_part = together(folded, col_part)
            folded = jnp.concatenate([folded, swap(folded, Z_STEPS[0])], 1)
        col_parts = exchange(col_part, COL_MASK)
        if step == 0:
            folded, col_parts = together(folded, col_parts)
        elif step == 1:
            quads[1], quads[3], col_parts = together(quads[1], quads[3], col_parts)
        elif step == 2:
            quads[2], col_parts = together(quads[2], col_parts)
        if step + 1 < ITERS:
            row_part = vmem_call(
                functools.partial(row_kernel, step + 1),
                shape((8, 8, 128)),
                inputs=2,
                nbytes=1024 * 1024,
            )(cost, col_parts)
    keep, log, send = vmem_call(
        target_kernel,
        (
            shape((4, rows, latent)),
            shape((4, rows, 128)),
            shape((4, rows, latent + 128), BF),
        ),
        scratch=[
            pltpu.VMEM((8 * rows, 16 * rows), BF),
            pltpu.VMEM((8, rows, latent), F32),
            pltpu.VMEM((8, rows, 128), F32),
        ],
        smem=1,
        inputs=3,
        flops=flops,
        nbytes=6 * 1024 * 1024,
    )(place, cost, data_all, col_parts)
    own, own_log, *sends = vmem_call(
        pair_kernel,
        (shape((rows, latent)), shape((rows, 128))) + (shape((rows, latent + 128), BF),) * 3,
        inputs=3,
        nbytes=2 * 1024 * 1024,
    )(keep, log, swap(send, CORE))
    others = [swap(value, mask) for value, mask in zip(sends, Z_STEPS)]
    return [own, own_log] + others, quads


def local(noise, data, t_index, embed_weight, position, norm_gain, qkv_weight):
    own = noise.shape[0]
    src, tgt = lax.axis_index("src"), lax.axis_index("tgt")
    ring = (src % 2) * 4 + tgt % 4
    place = jnp.stack([src // 2, tgt // 4, ring, tgt]).astype(jnp.int32)
    folded = folded_weights(embed_weight, position, norm_gain, qkv_weight)
    parts, quads = coupled_target(noise, data, place, folded)
    split, width = embed_weight.shape
    patch_count = position.shape[0]
    table = jnp.concatenate(
        [embed_weight, jnp.zeros_like(embed_weight), position, jnp.zeros_like(position)], 0
    )
    depth, columns = quads[0].shape
    columns = 4 * columns
    chunk = 256
    values = [*parts[:2], noise, t_index[:, None], table]
    far = [*parts[2:], *quads]
    qkv, velocity = pl.pallas_call(
        qkv_kernel,
        out_shape=(shape((own * patch_count, columns), BF), shape(noise.shape, BF)),
        grid_spec=pltpu.PrefetchScalarGridSpec(
            num_scalar_prefetch=1,
            grid=(own * patch_count // chunk,),
            in_specs=[pl.BlockSpec(value.shape, lambda j, where: (0, 0)) for value in values]
            + [pl.BlockSpec(memory_space=pltpu.HBM)] * len(far),
            out_specs=(
                pl.BlockSpec((chunk, columns), lambda j, where: (j, 0)),
                pl.BlockSpec(noise.shape, lambda j, where: (0, 0)),
            ),
            scratch_shapes=[pltpu.VMEM((own * patch_count, 2 * split), F32)]
            + [pltpu.VMEM(value.shape, BF) for value in far]
            + [pltpu.SemaphoreType.DMA((len(far),))],
        ),
        compiler_params=pltpu.CompilerParams(vmem_limit_bytes=58 * 1024 * 1024),
        cost_estimate=pl.CostEstimate(
            flops=2 * own * patch_count * depth * columns,
            bytes_accessed=16 * 1024 * 1024,
            transcendentals=0,
        ),
    )(place, *values, *far)
    return (velocity, qkv)


def solution(mesh):
    return jax.shard_map(
        local,
        mesh=mesh,
        in_specs=(
            P(("src", "tgt"), None),
            P(("src", "tgt"), None),
            P(("src", "tgt")),
            P(),
            P(),
            P(),
            P(None, "tgt"),
        ),
        out_specs=(P(("src", "tgt"), None), P(("src", "tgt"), None)),
        check_vma=False,
    )
```

```python
import functools

import jax
import jax.numpy as jnp
from jax import lax
from jax.experimental import pallas as pl
from jax.experimental.pallas import tpu as pltpu
from jax.sharding import PartitionSpec as P

ITERS = 3
TGRID = 1000
TILE = 1024
BOTH = ("src", "tgt")
CORE = 1
ROW_MASK, COL_MASK = 108, 19
Z_STEPS = (2, 16, 18)
Y_STEPS = (4, 8, 12)
X_STEPS = (32, 64, 96)
BF, F32 = jnp.bfloat16, jnp.float32


def epsilon_of(step):
    return 0.04 * 0.45**step


def swap(value, mask):
    return lax.ppermute(value, BOTH, [(i, i ^ mask) for i in range(128)])


def groups_by(mask):
    groups = {}
    for i in range(128):
        groups.setdefault(i & mask, []).append(i)
    return [groups[key] for key in sorted(groups)]


def exchange(value, mask):
    return lax.all_to_all(value, BOTH, 0, 0, axis_index_groups=groups_by(mask), tiled=True)


def vmem_call(kernel, out_shape, scratch=(), smem=0, inputs=0, flops=0, nbytes=0):
    return pl.pallas_call(
        kernel,
        out_shape=out_shape,
        in_specs=[pl.BlockSpec(memory_space=pltpu.SMEM)] * smem
        + [pl.BlockSpec(memory_space=pltpu.VMEM)] * inputs,
        out_specs=jax.tree.map(lambda _: pl.BlockSpec(memory_space=pltpu.VMEM), out_shape),
        scratch_shapes=list(scratch),
        compiler_params=pltpu.CompilerParams(vmem_limit_bytes=48 * 1024 * 1024),
        cost_estimate=pl.CostEstimate(flops=flops, bytes_accessed=nbytes, transcendentals=0),
    )


def shape(dims, dtype=F32):
    return jax.ShapeDtypeStruct(dims, dtype)


def eye(size):
    return lax.broadcasted_iota(jnp.int32, (size, size), 0) == lax.broadcasted_iota(
        jnp.int32, (size, size), 1
    )


def to_lanes(column):
    size = column.shape[0]
    wide = jnp.broadcast_to(column, (size, size))
    return jnp.sum(jnp.where(eye(size), wide, 0.0), axis=0, keepdims=True)


def to_rows(lanes):
    size = lanes.shape[1]
    wide = jnp.broadcast_to(lanes, (size, size))
    return jnp.sum(jnp.where(eye(size), wide, 0.0), axis=1, keepdims=True)


def join_lse(parts):
    peak = functools.reduce(jnp.maximum, parts)
    total = functools.reduce(jnp.add, [jnp.exp(part - peak) for part in parts])
    return peak + jnp.log(total)


def row_stats(cost_ref, col_pot, inverse):
    tiles = cost_ref.shape[1] // 128

    def score(tile):
        part = cost_ref[:, tile * 128 : (tile + 1) * 128]
        if col_pot is None:
            return -part * inverse
        return (col_pot[tile : tile + 1, :] - part) * inverse

    peak = score(0)
    for tile in range(1, tiles):
        peak = jnp.maximum(peak, score(tile))
    peak = jnp.max(peak, axis=1, keepdims=True)
    return score, peak


def row_lse(cost_ref, col_pot, inverse):
    score, peak = row_stats(cost_ref, col_pot, inverse)
    total = jnp.exp(score(0) - peak)
    for tile in range(1, cost_ref.shape[1] // 128):
        total = total + jnp.exp(score(tile) - peak)
    return peak + jnp.log(jnp.sum(total, axis=1, keepdims=True))


def pack(lse, out_ref):
    place = lax.broadcasted_iota(jnp.int32, (8, 128), 0)
    packed = jnp.zeros((8, 128), F32)
    for part in range(lse.shape[0] // 128):
        packed = jnp.where(place == part, to_lanes(lse[part * 128 : part * 128 + 128]), packed)
    out_ref[...] = jnp.broadcast_to(packed[None], out_ref.shape)


def spread_lse(parts):
    peak = jnp.max(parts, axis=0)
    return peak + jnp.log(jnp.sum(jnp.exp(parts - peak[None]), axis=0))


def cost_kernel(place, data_ref, a, b, c, d, cost_ref, lse_ref, noise_ref):
    h = place[2]
    rows, latent = a.shape[1:]
    for k, pair in enumerate((a, b, c, d)):
        noise_ref[h ^ (2 * k)] = pair[0]
        noise_ref[h ^ (2 * k + 1)] = pair[1]
    noise = noise_ref[...].reshape(8 * rows, latent)

    def square_sum(value):
        total = jnp.zeros((value.shape[0], 128), F32)
        for tile in range(latent // 128):
            part = value[:, tile * 128 : (tile + 1) * 128].astype(F32)
            total = total + part * part
        return jnp.sum(total, axis=1, keepdims=True)

    noise_sq = square_sum(noise)
    for group in range(2):
        part = data_ref[group * 8 : group * 8 + 8].reshape(8 * rows, latent)
        cross = lax.dot_general(
            noise, part, (((1,), (1,)), ((), ())), preferred_element_type=F32
        )
        for side in range(2):
            data_sq = to_lanes(square_sum(part[side * 128 : side * 128 + 128]))
            at = group * 256 + side * 128
            cost_ref[:, at : at + 128] = (
                noise_sq + data_sq - 2.0 * cross[:, side * 128 : side * 128 + 128]
            ) / latent
    pack(row_lse(cost_ref, None, 1.0 / epsilon_of(0)), lse_ref)


def col_kernel(step, cost_ref, parts_ref, out_ref):
    epsilon = epsilon_of(step)
    joined = -epsilon * spread_lse(parts_ref[...])
    halfway = cost_ref.shape[0] // 2
    inverse = 1.0 / epsilon
    upper = (to_rows(joined[0:1, :]) - cost_ref[0:halfway, :]) * inverse
    lower = (to_rows(joined[1:2, :]) - cost_ref[halfway : 2 * halfway, :]) * inverse
    peak = jnp.maximum(
        jnp.max(upper, axis=0, keepdims=True), jnp.max(lower, axis=0, keepdims=True)
    )
    total = jnp.sum(jnp.exp(upper - peak) + jnp.exp(lower - peak), axis=0, keepdims=True)
    lse = peak + jnp.log(total)
    place = lax.broadcasted_iota(jnp.int32, (8, 128), 0)
    packed = jnp.zeros((8, 128), F32)
    for tile in range(lse.shape[1] // 128):
        packed = jnp.where(place == tile, lse[:, tile * 128 : (tile + 1) * 128], packed)
    out_ref[...] = jnp.broadcast_to(packed[None], out_ref.shape)


def col_potential(step, parts_ref):
    return -epsilon_of(step) * spread_lse(parts_ref[...])


def row_kernel(step, cost_ref, parts_ref, lse_ref):
    pack(row_lse(cost_ref, col_potential(step - 1, parts_ref), 1.0 / epsilon_of(step)), lse_ref)


def packed_log(value):
    lane = lax.broadcasted_iota(jnp.int32, value.shape, 1)
    high = value.astype(BF).astype(F32)
    middle = (value - high).astype(BF).astype(F32)
    low = value - high - middle
    return jnp.where(
        lane == 0, high, jnp.where(lane == 1, middle, jnp.where(lane == 2, low, 0.0))
    ).astype(BF)


def target_kernel(place, cost_ref, data_ref, parts_ref, keep_ref, log_ref, send_ref, coupling, sums, lses):
    h = place[2]
    col_pot = col_potential(ITERS - 1, parts_ref)
    score, peak = row_stats(cost_ref, col_pot, 1.0 / epsilon_of(ITERS - 1))
    total = jnp.zeros(cost_ref.shape[:1] + (128,), F32)
    for tile in range(cost_ref.shape[1] // 128):
        expo = jnp.exp(score(tile) - peak)
        total = total + expo
        coupling[:, tile * 128 : (tile + 1) * 128] = expo.astype(BF)
    denom = jnp.sum(total, axis=1, keepdims=True)
    count, rows, latent = sums.shape
    lses[...] = jnp.broadcast_to(peak + jnp.log(denom), (count * rows, 128)).reshape(lses.shape)
    share = 1.0 / denom
    for at in range(0, latent, 512):
        part = data_ref[:, :, at : at + 512].reshape(-1, 512)
        product = jnp.dot(coupling[...], part, preferred_element_type=F32) * share
        sums[:, :, at : at + 512] = product.reshape(count, rows, 512)
    for k in range(4):
        keep_ref[k] = sums[h ^ (2 * k)]
        log_ref[k] = lses[h ^ (2 * k)]
        send_ref[k, :, 0:latent] = sums[h ^ (2 * k + 1)].astype(BF)
        send_ref[k, :, latent : latent + 128] = packed_log(lses[h ^ (2 * k + 1)])


def read_log(ref_value):
    return jnp.sum(ref_value.astype(F32), axis=1, keepdims=True)


def pair_kernel(keep_ref, log_ref, got_ref, own_ref, own_log_ref, s1, s2, s3):
    latent = keep_ref.shape[2]
    for k, out in enumerate((own_ref, s1, s2, s3)):
        first = log_ref[k]
        second = jnp.broadcast_to(read_log(got_ref[k, :, latent : latent + 128]), first.shape)
        total = join_lse([first, second])
        mixed = keep_ref[k] * jnp.exp(first - total)[:, 0:1] + got_ref[
            k, :, 0:latent
        ].astype(F32) * jnp.exp(second - total)[:, 0:1]
        if k == 0:
            out[...] = mixed
            own_log_ref[...] = total
        else:
            out[:, 0:latent] = mixed.astype(BF)
            out[:, latent : latent + 128] = packed_log(total)


def spread_kernel(value_ref, out_ref, sems):
    copies = [
        pltpu.make_async_copy(value_ref, out_ref.at[k], sems.at[k])
        for k in range(out_ref.shape[0])
    ]
    for copy in copies:
        copy.start()
    for copy in copies:
        copy.wait()


def qkv_kernel(
    place, own_ref, log_ref, noise_ref, time_ref, table_ref, *refs
):
    far = refs[:7]
    out_ref, velocity_ref, tokens = refs[7:10]
    a, b, c, folded, sems = refs[10:15]
    rows, latent = own_ref.shape
    step = pl.program_id(0)

    @pl.when(step == 0)
    def _():
        copies = [
            pltpu.make_async_copy(there, here, sems.at[k])
            for k, (there, here) in enumerate(zip(far, (a, b, c)))
        ]
        for k in range(16):
            columns = folded.shape[1] // 16
            to = pl.multiple_of((place[3] ^ k) * columns, 128)
            copies.append(
                pltpu.make_async_copy(
                    far[3 + k // 4].at[:, pl.ds((k % 4) * columns, columns)],
                    folded.at[:, pl.ds(to, columns)],
                    sems.at[3 + k],
                )
            )
        for copy in copies:
            copy.start()
        for copy in copies[:3]:
            copy.wait()
        logs = [log_ref[...]] + [
            jnp.broadcast_to(read_log(got[:, latent : latent + 128]), log_ref.shape)
            for got in (a, b, c)
        ]
        total = join_lse(logs)
        shares = [jnp.exp(log - total) for log in logs]
        times = jnp.broadcast_to(time_ref[...].astype(F32) / TGRID, (rows, 128))
        first = lax.broadcasted_iota(jnp.int32, (rows, 128), 1) < 64
        for tile in range(latent // 128):
            cut = slice(tile * 128, tile * 128 + 128)
            target = own_ref[:, cut] * shares[0]
            for got, share in zip((a, b, c), shares[1:]):
                target = target + got[:, cut].astype(F32) * share
            noise = noise_ref[:, cut].astype(F32)
            velocity_ref[:, cut] = (target - noise).astype(BF)
            mixed = ((1.0 - times) * noise + times * target).astype(BF).astype(F32)
            turned = pltpu.roll(mixed, 64, 1)
            tokens[pl.ds(2 * tile, rows, stride=latent // 64), :] = jnp.where(
                first, mixed, turned
            )
            tokens[pl.ds(2 * tile + 1, rows, stride=latent // 64), :] = jnp.where(
                first, turned, mixed
            )
        for copy in copies[3:]:
            copy.wait()

    count = out_ref.shape[0]
    width = table_ref.shape[1]
    patches = tokens[pl.ds(pl.multiple_of(step * count, count), count), :].astype(BF)
    spot = lax.broadcasted_iota(jnp.int32, (count, 128), 0) % 32
    lane = lax.broadcasted_iota(jnp.int32, (count, 128), 1)
    spots = jnp.where(spot == lane % 32, 1.0, 0.0).astype(BF)
    chunk = jnp.concatenate([patches, spots[:, 0:64]], axis=1)
    total = jnp.zeros((count, 128), F32)
    for col in range(0, width, 256):
        part = jnp.dot(chunk, table_ref[:, col : col + 256], preferred_element_type=F32)
        part = part * part
        total = total + part[:, 0:128] + part[:, 128:256]
    scale = lax.rsqrt(jnp.sum(total, axis=1, keepdims=True) / width + 1e-06)
    for at in range(0, folded.shape[1], TILE):
        product = jnp.dot(chunk, folded[:, at : at + TILE], preferred_element_type=F32)
        out_ref[:, at : at + TILE] = (product * scale).astype(BF)


def halves(value):
    high = value.astype(BF)
    low = (value - high.astype(F32)).astype(BF)
    return high, low


def folded_weights(embed_weight, position, norm_gain, qkv_weight):
    scaled = jnp.concatenate([embed_weight, position], 0).astype(F32) * norm_gain
    high, low = halves(scaled)
    both = jnp.dot(jnp.concatenate([high, low], 0), qkv_weight, preferred_element_type=F32)
    rows = scaled.shape[0]
    high, low = halves(both[:rows] + both[rows:])
    split = embed_weight.shape[0]
    return jnp.concatenate([high[:split], low[:split], high[split:], low[split:]], 0)


def together(*values):
    return lax.optimization_barrier(values)


def coupled_target(noise, data, place, folded):
    rows, latent = noise.shape
    noise_pair = jnp.stack([noise, swap(noise, CORE)])
    noises = [noise_pair] + [swap(noise_pair, mask) for mask in Z_STEPS]
    spread = pl.pallas_call(
        spread_kernel,
        out_shape=shape((16, rows, latent), BF),
        in_specs=[pl.BlockSpec(memory_space=pltpu.VMEM)],
        out_specs=pl.BlockSpec(memory_space=pl.ANY),
        scratch_shapes=[pltpu.SemaphoreType.DMA((16,))],
    )(data)
    data_all = exchange(spread, COL_MASK)
    flops = 2 * 8 * rows * 16 * rows * latent
    cost, row_part = vmem_call(
        cost_kernel,
        (shape((8 * rows, 16 * rows)), shape((8, 8, 128))),
        scratch=[pltpu.VMEM((8, rows, latent), BF)],
        smem=1,
        inputs=5,
        flops=flops,
        nbytes=4 * 1024 * 1024,
    )(place, data_all, *noises)
    quads = [None] * 4
    folded, row_part = together(folded, row_part)
    folded = jnp.concatenate([folded, swap(folded, CORE)], 1)
    for step in range(ITERS):
        if step == 1:
            folded, row_part = together(folded, row_part)
            quads = [folded, swap(folded, Y_STEPS[0]), None, swap(folded, Y_STEPS[2])]
        elif step == 2:
            folded, row_part = together(folded, row_part)
            quads[2] = swap(folded, Y_STEPS[1])
        row_parts = exchange(row_part, ROW_MASK)
        col_part = vmem_call(
            functools.partial(col_kernel, step), shape((16, 8, 128)), inputs=2, nbytes=1024 * 1024
        )(cost, row_parts)
        if step == 0:
            folded, col_part = together(folded, col_part)
            folded = jnp.concatenate([folded, swap(folded, Z_STEPS[0])], 1)
        col_parts = exchange(col_part, COL_MASK)
        if step == 0:
            folded, col_parts = together(folded, col_parts)
        elif step == 1:
            quads[1], quads[3], col_parts = together(quads[1], quads[3], col_parts)
        elif step == 2:
            quads[2], col_parts = together(quads[2], col_parts)
        if step + 1 < ITERS:
            row_part = vmem_call(
                functools.partial(row_kernel, step + 1),
                shape((8, 8, 128)),
                inputs=2,
                nbytes=1024 * 1024,
            )(cost, col_parts)
    keep, log, send = vmem_call(
        target_kernel,
        (
            shape((4, rows, latent)),
            shape((4, rows, 128)),
            shape((4, rows, latent + 128), BF),
        ),
        scratch=[
            pltpu.VMEM((8 * rows, 16 * rows), BF),
            pltpu.VMEM((8, rows, latent), F32),
            pltpu.VMEM((8, rows, 128), F32),
        ],
        smem=1,
        inputs=3,
        flops=flops,
        nbytes=6 * 1024 * 1024,
    )(place, cost, data_all, col_parts)
    own, own_log, *sends = vmem_call(
        pair_kernel,
        (shape((rows, latent)), shape((rows, 128))) + (shape((rows, latent + 128), BF),) * 3,
        inputs=3,
        nbytes=2 * 1024 * 1024,
    )(keep, log, swap(send, CORE))
    others = [swap(value, mask) for value, mask in zip(sends, Z_STEPS)]
    return [own, own_log] + others, quads


def local(noise, data, t_index, embed_weight, position, norm_gain, qkv_weight):
    own = noise.shape[0]
    src, tgt = lax.axis_index("src"), lax.axis_index("tgt")
    ring = (src % 2) * 4 + tgt % 4
    place = jnp.stack([src // 2, tgt // 4, ring, tgt]).astype(jnp.int32)
    folded = folded_weights(embed_weight, position, norm_gain, qkv_weight)
    parts, quads = coupled_target(noise, data, place, folded)
    split, width = embed_weight.shape
    patch_count = position.shape[0]
    table = jnp.concatenate(
        [embed_weight, jnp.zeros_like(embed_weight), position, jnp.zeros_like(position)], 0
    )
    depth, columns = quads[0].shape
    columns = 4 * columns
    chunk = 256
    values = [*parts[:2], noise, t_index[:, None], table]
    far = [*parts[2:], *quads]
    qkv, velocity = pl.pallas_call(
        qkv_kernel,
        out_shape=(shape((own * patch_count, columns), BF), shape(noise.shape, BF)),
        grid_spec=pltpu.PrefetchScalarGridSpec(
            num_scalar_prefetch=1,
            grid=(own * patch_count // chunk,),
            in_specs=[pl.BlockSpec(value.shape, lambda j, where: (0, 0)) for value in values]
            + [pl.BlockSpec(memory_space=pltpu.HBM)] * len(far),
            out_specs=(
                pl.BlockSpec((chunk, columns), lambda j, where: (j, 0)),
                pl.BlockSpec(noise.shape, lambda j, where: (0, 0)),
            ),
            scratch_shapes=[pltpu.VMEM((own * patch_count, 2 * split), F32)]
            + [pltpu.VMEM(value.shape, BF) for value in far[:3]]
            + [pltpu.VMEM((depth, columns), BF), pltpu.SemaphoreType.DMA((19,))],
        ),
        compiler_params=pltpu.CompilerParams(vmem_limit_bytes=53 * 1024 * 1024),
        cost_estimate=pl.CostEstimate(
            flops=2 * own * patch_count * depth * columns,
            bytes_accessed=16 * 1024 * 1024,
            transcendentals=0,
        ),
    )(place, *values, *far)
    return (velocity, qkv)


def solution(mesh):
    return jax.shard_map(
        local,
        mesh=mesh,
        in_specs=(
            P(("src", "tgt"), None),
            P(("src", "tgt"), None),
            P(("src", "tgt")),
            P(),
            P(),
            P(),
            P(None, "tgt"),
        ),
        out_specs=(P(("src", "tgt"), None), P(("src", "tgt"), None)),
        check_vma=False,
    )
```

```python
import functools

import jax
import jax.numpy as jnp
from jax import lax
from jax.experimental import pallas as pl
from jax.experimental.pallas import tpu as pltpu
from jax.sharding import PartitionSpec as P

ITERS = 3
TGRID = 1000
TILE = 1024
BOTH = ("src", "tgt")
CORE = 1
ROW_MASK, COL_MASK = 108, 19
Z_STEPS = (2, 16, 18)
Y_STEPS = (4, 8, 12)
X_STEPS = (32, 64, 96)
BF, F32 = jnp.bfloat16, jnp.float32


def epsilon_of(step):
    return 0.04 * 0.45**step


def swap(value, mask):
    return lax.ppermute(value, BOTH, [(i, i ^ mask) for i in range(128)])


def groups_by(mask):
    groups = {}
    for i in range(128):
        groups.setdefault(i & mask, []).append(i)
    return [groups[key] for key in sorted(groups)]


def exchange(value, mask):
    return lax.all_to_all(value, BOTH, 0, 0, axis_index_groups=groups_by(mask), tiled=True)


def vmem_call(kernel, out_shape, scratch=(), smem=0, inputs=0, flops=0, nbytes=0):
    return pl.pallas_call(
        kernel,
        out_shape=out_shape,
        in_specs=[pl.BlockSpec(memory_space=pltpu.SMEM)] * smem
        + [pl.BlockSpec(memory_space=pltpu.VMEM)] * inputs,
        out_specs=jax.tree.map(lambda _: pl.BlockSpec(memory_space=pltpu.VMEM), out_shape),
        scratch_shapes=list(scratch),
        compiler_params=pltpu.CompilerParams(vmem_limit_bytes=48 * 1024 * 1024),
        cost_estimate=pl.CostEstimate(flops=flops, bytes_accessed=nbytes, transcendentals=0),
    )


def shape(dims, dtype=F32):
    return jax.ShapeDtypeStruct(dims, dtype)


def eye(size):
    return lax.broadcasted_iota(jnp.int32, (size, size), 0) == lax.broadcasted_iota(
        jnp.int32, (size, size), 1
    )


def to_lanes(column):
    size = column.shape[0]
    wide = jnp.broadcast_to(column, (size, size))
    return jnp.sum(jnp.where(eye(size), wide, 0.0), axis=0, keepdims=True)


def to_rows(lanes):
    size = lanes.shape[1]
    wide = jnp.broadcast_to(lanes, (size, size))
    return jnp.sum(jnp.where(eye(size), wide, 0.0), axis=1, keepdims=True)


def join_lse(parts):
    peak = functools.reduce(jnp.maximum, parts)
    total = functools.reduce(jnp.add, [jnp.exp(part - peak) for part in parts])
    return peak + jnp.log(total)


def row_stats(cost_ref, col_pot, inverse):
    tiles = cost_ref.shape[1] // 128

    def score(tile):
        part = cost_ref[:, tile * 128 : (tile + 1) * 128]
        if col_pot is None:
            return -part * inverse
        return (col_pot[tile : tile + 1, :] - part) * inverse

    peak = score(0)
    for tile in range(1, tiles):
        peak = jnp.maximum(peak, score(tile))
    peak = jnp.max(peak, axis=1, keepdims=True)
    return score, peak


def row_lse(cost_ref, col_pot, inverse):
    score, peak = row_stats(cost_ref, col_pot, inverse)
    total = jnp.exp(score(0) - peak)
    for tile in range(1, cost_ref.shape[1] // 128):
        total = total + jnp.exp(score(tile) - peak)
    return peak + jnp.log(jnp.sum(total, axis=1, keepdims=True))


def pack(lse, out_ref):
    place = lax.broadcasted_iota(jnp.int32, (8, 128), 0)
    packed = jnp.zeros((8, 128), F32)
    for part in range(lse.shape[0] // 128):
        packed = jnp.where(place == part, to_lanes(lse[part * 128 : part * 128 + 128]), packed)
    out_ref[...] = jnp.broadcast_to(packed[None], out_ref.shape)


def spread_lse(parts):
    peak = jnp.max(parts, axis=0)
    return peak + jnp.log(jnp.sum(jnp.exp(parts - peak[None]), axis=0))


def square_sum(value):
    total = jnp.zeros((value.shape[0], 128), F32)
    for tile in range(value.shape[1] // 128):
        part = value[:, tile * 128 : (tile + 1) * 128].astype(F32)
        total = total + part * part
    return jnp.sum(total, axis=1, keepdims=True)


def noise_kernel(place, a, b, c, d, noise_ref, square_ref):
    h = place[2]
    rows, latent = a.shape[1:]
    for k, pair in enumerate((a, b, c, d)):
        noise_ref[h ^ (2 * k)] = pair[0]
        noise_ref[h ^ (2 * k + 1)] = pair[1]
    squares = square_sum(noise_ref[...].reshape(8 * rows, latent))
    square_ref[...] = jnp.broadcast_to(squares, square_ref.shape)


def cost_kernel(data_ref, noise_ref, square_ref, cost_ref, lse_ref):
    rows, latent = noise_ref.shape[1:]
    noise = noise_ref[...].reshape(8 * rows, latent)

    for group in range(2):
        part = data_ref[group * 8 : group * 8 + 8].reshape(8 * rows, latent)
        cross = lax.dot_general(
            noise, part, (((1,), (1,)), ((), ())), preferred_element_type=F32
        )
        for side in range(2):
            data_sq = to_lanes(square_sum(part[side * 128 : side * 128 + 128]))
            at = group * 256 + side * 128
            cost_ref[:, at : at + 128] = (
                square_ref[...] + data_sq - 2.0 * cross[:, side * 128 : side * 128 + 128]
            ) / latent
    pack(row_lse(cost_ref, None, 1.0 / epsilon_of(0)), lse_ref)


def col_kernel(step, cost_ref, parts_ref, out_ref):
    epsilon = epsilon_of(step)
    joined = -epsilon * spread_lse(parts_ref[...])
    halfway = cost_ref.shape[0] // 2
    inverse = 1.0 / epsilon
    upper = (to_rows(joined[0:1, :]) - cost_ref[0:halfway, :]) * inverse
    lower = (to_rows(joined[1:2, :]) - cost_ref[halfway : 2 * halfway, :]) * inverse
    peak = jnp.maximum(
        jnp.max(upper, axis=0, keepdims=True), jnp.max(lower, axis=0, keepdims=True)
    )
    total = jnp.sum(jnp.exp(upper - peak) + jnp.exp(lower - peak), axis=0, keepdims=True)
    lse = peak + jnp.log(total)
    place = lax.broadcasted_iota(jnp.int32, (8, 128), 0)
    packed = jnp.zeros((8, 128), F32)
    for tile in range(lse.shape[1] // 128):
        packed = jnp.where(place == tile, lse[:, tile * 128 : (tile + 1) * 128], packed)
    out_ref[...] = jnp.broadcast_to(packed[None], out_ref.shape)


def col_potential(step, parts_ref):
    return -epsilon_of(step) * spread_lse(parts_ref[...])


def row_kernel(step, cost_ref, parts_ref, lse_ref):
    pack(row_lse(cost_ref, col_potential(step - 1, parts_ref), 1.0 / epsilon_of(step)), lse_ref)


def packed_log(value):
    lane = lax.broadcasted_iota(jnp.int32, value.shape, 1)
    high = value.astype(BF).astype(F32)
    middle = (value - high).astype(BF).astype(F32)
    low = value - high - middle
    return jnp.where(
        lane == 0, high, jnp.where(lane == 1, middle, jnp.where(lane == 2, low, 0.0))
    ).astype(BF)


def target_kernel(place, cost_ref, data_ref, parts_ref, keep_ref, log_ref, send_ref, coupling, sums, lses):
    h = place[2]
    col_pot = col_potential(ITERS - 1, parts_ref)
    score, peak = row_stats(cost_ref, col_pot, 1.0 / epsilon_of(ITERS - 1))
    total = jnp.zeros(cost_ref.shape[:1] + (128,), F32)
    for tile in range(cost_ref.shape[1] // 128):
        expo = jnp.exp(score(tile) - peak)
        total = total + expo
        coupling[:, tile * 128 : (tile + 1) * 128] = expo.astype(BF)
    denom = jnp.sum(total, axis=1, keepdims=True)
    count, rows, latent = sums.shape
    lses[...] = jnp.broadcast_to(peak + jnp.log(denom), (count * rows, 128)).reshape(lses.shape)
    share = 1.0 / denom
    for at in range(0, latent, 512):
        part = data_ref[:, :, at : at + 512].reshape(-1, 512)
        product = jnp.dot(coupling[...], part, preferred_element_type=F32) * share
        sums[:, :, at : at + 512] = product.reshape(count, rows, 512)
    for k in range(4):
        keep_ref[k] = sums[h ^ (2 * k)]
        log_ref[k] = lses[h ^ (2 * k)]
        send_ref[k, :, 0:latent] = sums[h ^ (2 * k + 1)].astype(BF)
        send_ref[k, :, latent : latent + 128] = packed_log(lses[h ^ (2 * k + 1)])


def read_log(ref_value):
    return jnp.sum(ref_value.astype(F32), axis=1, keepdims=True)


def pair_parts(keep_ref, log_ref, got_ref, k):
    latent = keep_ref.shape[2]
    first = log_ref[k]
    second = jnp.broadcast_to(read_log(got_ref[k, :, latent : latent + 128]), first.shape)
    total = join_lse([first, second])
    mixed = keep_ref[k] * jnp.exp(first - total)[:, 0:1] + got_ref[k, :, 0:latent].astype(
        F32
    ) * jnp.exp(second - total)[:, 0:1]
    return mixed, total


def pair_send(keep_ref, log_ref, got_ref, k, out):
    latent = keep_ref.shape[2]
    mixed, total = pair_parts(keep_ref, log_ref, got_ref, k)
    out[:, 0:latent] = mixed.astype(BF)
    out[:, latent : latent + 128] = packed_log(total)


def far_kernel(keep_ref, log_ref, got_ref, out):
    pair_send(keep_ref, log_ref, got_ref, 2, out)


def pair_kernel(keep_ref, log_ref, got_ref, own_ref, own_log_ref, s1, s3):
    own_ref[...], own_log_ref[...] = pair_parts(keep_ref, log_ref, got_ref, 0)
    pair_send(keep_ref, log_ref, got_ref, 1, s1)
    pair_send(keep_ref, log_ref, got_ref, 3, s3)


def spread_kernel(value_ref, out_ref, sems):
    copies = [
        pltpu.make_async_copy(value_ref, out_ref.at[k], sems.at[k])
        for k in range(out_ref.shape[0])
    ]
    for copy in copies:
        copy.start()
    for copy in copies:
        copy.wait()


def qkv_kernel(
    place, own_ref, log_ref, noise_ref, time_ref, table_ref, *refs
):
    far = refs[:7]
    out_ref, velocity_ref, tokens = refs[7:10]
    a, b, c, folded, sems = refs[10:15]
    rows, latent = own_ref.shape
    step = pl.program_id(0)

    @pl.when(step == 0)
    def _():
        copies = [
            pltpu.make_async_copy(there, here, sems.at[k])
            for k, (there, here) in enumerate(zip(far, (a, b, c)))
        ]
        for k in range(16):
            columns = folded.shape[1] // 16
            to = pl.multiple_of((place[3] ^ k) * columns, 128)
            copies.append(
                pltpu.make_async_copy(
                    far[3 + k // 4].at[:, pl.ds((k % 4) * columns, columns)],
                    folded.at[:, pl.ds(to, columns)],
                    sems.at[3 + k],
                )
            )
        for copy in copies:
            copy.start()
        for copy in copies[:3]:
            copy.wait()
        logs = [log_ref[...]] + [
            jnp.broadcast_to(read_log(got[:, latent : latent + 128]), log_ref.shape)
            for got in (a, b, c)
        ]
        total = join_lse(logs)
        shares = [jnp.exp(log - total) for log in logs]
        times = jnp.broadcast_to(time_ref[...].astype(F32) / TGRID, (rows, 128))
        first = lax.broadcasted_iota(jnp.int32, (rows, 128), 1) < 64
        for tile in range(latent // 128):
            cut = slice(tile * 128, tile * 128 + 128)
            target = own_ref[:, cut] * shares[0]
            for got, share in zip((a, b, c), shares[1:]):
                target = target + got[:, cut].astype(F32) * share
            noise = noise_ref[:, cut].astype(F32)
            velocity_ref[:, cut] = (target - noise).astype(BF)
            mixed = ((1.0 - times) * noise + times * target).astype(BF).astype(F32)
            turned = pltpu.roll(mixed, 64, 1)
            tokens[pl.ds(2 * tile, rows, stride=latent // 64), :] = jnp.where(
                first, mixed, turned
            )
            tokens[pl.ds(2 * tile + 1, rows, stride=latent // 64), :] = jnp.where(
                first, turned, mixed
            )
        for copy in copies[3:]:
            copy.wait()

    count = out_ref.shape[0]
    width = table_ref.shape[1]
    patches = tokens[pl.ds(pl.multiple_of(step * count, count), count), :].astype(BF)
    spot = lax.broadcasted_iota(jnp.int32, (count, 128), 0) % 32
    lane = lax.broadcasted_iota(jnp.int32, (count, 128), 1)
    spots = jnp.where(spot == lane % 32, 1.0, 0.0).astype(BF)
    chunk = jnp.concatenate([patches, spots[:, 0:64]], axis=1)
    total = jnp.zeros((count, 128), F32)
    for col in range(0, width, 256):
        part = jnp.dot(chunk, table_ref[:, col : col + 256], preferred_element_type=F32)
        part = part * part
        total = total + part[:, 0:128] + part[:, 128:256]
    scale = lax.rsqrt(jnp.sum(total, axis=1, keepdims=True) / width + 1e-06)
    for at in range(0, folded.shape[1], TILE):
        product = jnp.dot(chunk, folded[:, at : at + TILE], preferred_element_type=F32)
        out_ref[:, at : at + TILE] = (product * scale).astype(BF)


def halves(value):
    high = value.astype(BF)
    low = (value - high.astype(F32)).astype(BF)
    return high, low


def folded_weights(embed_weight, position, norm_gain, qkv_weight):
    scaled = jnp.concatenate([embed_weight, position], 0).astype(F32) * norm_gain
    high, low = halves(scaled)
    both = jnp.dot(jnp.concatenate([high, low], 0), qkv_weight, preferred_element_type=F32)
    rows = scaled.shape[0]
    high, low = halves(both[:rows] + both[rows:])
    split = embed_weight.shape[0]
    return jnp.concatenate([high[:split], low[:split], high[split:], low[split:]], 0)


def together(*values):
    return lax.optimization_barrier(values)


def coupled_target(noise, data, place, folded):
    rows, latent = noise.shape
    noise_pair = jnp.stack([noise, swap(noise, CORE)])
    noises = [noise_pair] + [swap(noise_pair, mask) for mask in Z_STEPS]
    spread = pl.pallas_call(
        spread_kernel,
        out_shape=shape((16, rows, latent), BF),
        in_specs=[pl.BlockSpec(memory_space=pltpu.VMEM)],
        out_specs=pl.BlockSpec(memory_space=pl.ANY),
        scratch_shapes=[pltpu.SemaphoreType.DMA((16,))],
    )(data)
    data_all = exchange(spread, COL_MASK)
    flops = 2 * 8 * rows * 16 * rows * latent
    noise_all, squares = vmem_call(
        noise_kernel,
        (shape((8, rows, latent), BF), shape((8 * rows, 128))),
        smem=1,
        inputs=4,
        nbytes=2 * 1024 * 1024,
    )(place, *noises)
    cost, row_part = vmem_call(
        cost_kernel,
        (shape((8 * rows, 16 * rows)), shape((8, 8, 128))),
        inputs=3,
        flops=flops,
        nbytes=4 * 1024 * 1024,
    )(data_all, noise_all, squares)
    quads = [None] * 4
    folded, row_part = together(folded, row_part)
    folded = jnp.concatenate([folded, swap(folded, CORE)], 1)
    for step in range(ITERS):
        if step == 1:
            folded, row_part = together(folded, row_part)
            quads = [folded, swap(folded, Y_STEPS[0]), None, swap(folded, Y_STEPS[2])]
        elif step == 2:
            folded, row_part = together(folded, row_part)
            quads[2] = swap(folded, Y_STEPS[1])
        row_parts = exchange(row_part, ROW_MASK)
        col_part = vmem_call(
            functools.partial(col_kernel, step), shape((16, 8, 128)), inputs=2, nbytes=1024 * 1024
        )(cost, row_parts)
        if step == 0:
            folded, col_part = together(folded, col_part)
            folded = jnp.concatenate([folded, swap(folded, Z_STEPS[0])], 1)
        col_parts = exchange(col_part, COL_MASK)
        if step == 0:
            folded, col_parts = together(folded, col_parts)
        elif step == 1:
            quads[1], quads[3], col_parts = together(quads[1], quads[3], col_parts)
        elif step == 2:
            quads[2], col_parts = together(quads[2], col_parts)
        if step + 1 < ITERS:
            row_part = vmem_call(
                functools.partial(row_kernel, step + 1),
                shape((8, 8, 128)),
                inputs=2,
                nbytes=1024 * 1024,
            )(cost, col_parts)
    keep, log, send = vmem_call(
        target_kernel,
        (
            shape((4, rows, latent)),
            shape((4, rows, 128)),
            shape((4, rows, latent + 128), BF),
        ),
        scratch=[
            pltpu.VMEM((8 * rows, 16 * rows), BF),
            pltpu.VMEM((8, rows, latent), F32),
            pltpu.VMEM((8, rows, 128), F32),
        ],
        smem=1,
        inputs=3,
        flops=flops,
        nbytes=6 * 1024 * 1024,
    )(place, cost, data_all, col_parts)
    got = swap(send, CORE)
    message = shape((rows, latent + 128), BF)
    far_send = vmem_call(far_kernel, message, inputs=3, nbytes=1024 * 1024)(keep, log, got)
    far_send, keep = together(far_send, keep)
    own, own_log, *sends = vmem_call(
        pair_kernel,
        (shape((rows, latent)), shape((rows, 128)), message, message),
        inputs=3,
        nbytes=2 * 1024 * 1024,
    )(keep, log, got)
    others = [swap(sends[0], Z_STEPS[0]), swap(far_send, Z_STEPS[1]), swap(sends[1], Z_STEPS[2])]
    return [own, own_log] + others, quads


def local(noise, data, t_index, embed_weight, position, norm_gain, qkv_weight):
    own = noise.shape[0]
    src, tgt = lax.axis_index("src"), lax.axis_index("tgt")
    ring = (src % 2) * 4 + tgt % 4
    place = jnp.stack([src // 2, tgt // 4, ring, tgt]).astype(jnp.int32)
    folded = folded_weights(embed_weight, position, norm_gain, qkv_weight)
    parts, quads = coupled_target(noise, data, place, folded)
    split, width = embed_weight.shape
    patch_count = position.shape[0]
    table = jnp.concatenate(
        [embed_weight, jnp.zeros_like(embed_weight), position, jnp.zeros_like(position)], 0
    )
    depth, columns = quads[0].shape
    columns = 4 * columns
    chunk = 256
    values = [*parts[:2], noise, t_index[:, None], table]
    far = [*parts[2:], *quads]
    qkv, velocity = pl.pallas_call(
        qkv_kernel,
        out_shape=(shape((own * patch_count, columns), BF), shape(noise.shape, BF)),
        grid_spec=pltpu.PrefetchScalarGridSpec(
            num_scalar_prefetch=1,
            grid=(own * patch_count // chunk,),
            in_specs=[pl.BlockSpec(value.shape, lambda j, where: (0, 0)) for value in values]
            + [pl.BlockSpec(memory_space=pltpu.HBM)] * len(far),
            out_specs=(
                pl.BlockSpec((chunk, columns), lambda j, where: (j, 0)),
                pl.BlockSpec(noise.shape, lambda j, where: (0, 0)),
            ),
            scratch_shapes=[pltpu.VMEM((own * patch_count, 2 * split), F32)]
            + [pltpu.VMEM(value.shape, BF) for value in far[:3]]
            + [pltpu.VMEM((depth, columns), BF), pltpu.SemaphoreType.DMA((19,))],
        ),
        compiler_params=pltpu.CompilerParams(vmem_limit_bytes=53 * 1024 * 1024),
        cost_estimate=pl.CostEstimate(
            flops=2 * own * patch_count * depth * columns,
            bytes_accessed=16 * 1024 * 1024,
            transcendentals=0,
        ),
    )(place, *values, *far)
    return (velocity, qkv)


def solution(mesh):
    return jax.shard_map(
        local,
        mesh=mesh,
        in_specs=(
            P(("src", "tgt"), None),
            P(("src", "tgt"), None),
            P(("src", "tgt")),
            P(),
            P(),
            P(),
            P(None, "tgt"),
        ),
        out_specs=(P(("src", "tgt"), None), P(("src", "tgt"), None)),
        check_vma=False,
    )
```

```python
import functools

import jax
import jax.numpy as jnp
from jax import lax
from jax.experimental import pallas as pl
from jax.experimental.pallas import tpu as pltpu
from jax.sharding import PartitionSpec as P

ITERS = 3
TGRID = 1000
TILE = 1024
BOTH = ("src", "tgt")
CORE = 1
ROW_MASK, COL_MASK = 108, 19
Z_STEPS = (2, 16, 18)
Y_STEPS = (4, 8, 12)
X_STEPS = (32, 64, 96)
BF, F32 = jnp.bfloat16, jnp.float32


def epsilon_of(step):
    return 0.04 * 0.45**step


def swap(value, mask):
    return lax.ppermute(value, BOTH, [(i, i ^ mask) for i in range(128)])


def groups_by(mask):
    groups = {}
    for i in range(128):
        groups.setdefault(i & mask, []).append(i)
    return [groups[key] for key in sorted(groups)]


def exchange(value, mask):
    return lax.all_to_all(value, BOTH, 0, 0, axis_index_groups=groups_by(mask), tiled=True)


def vmem_call(kernel, out_shape, scratch=(), smem=0, inputs=0, flops=0, nbytes=0):
    return pl.pallas_call(
        kernel,
        out_shape=out_shape,
        in_specs=[pl.BlockSpec(memory_space=pltpu.SMEM)] * smem
        + [pl.BlockSpec(memory_space=pltpu.VMEM)] * inputs,
        out_specs=jax.tree.map(lambda _: pl.BlockSpec(memory_space=pltpu.VMEM), out_shape),
        scratch_shapes=list(scratch),
        compiler_params=pltpu.CompilerParams(vmem_limit_bytes=48 * 1024 * 1024),
        cost_estimate=pl.CostEstimate(flops=flops, bytes_accessed=nbytes, transcendentals=0),
    )


def shape(dims, dtype=F32):
    return jax.ShapeDtypeStruct(dims, dtype)


def eye(size):
    return lax.broadcasted_iota(jnp.int32, (size, size), 0) == lax.broadcasted_iota(
        jnp.int32, (size, size), 1
    )


def to_lanes(column):
    size = column.shape[0]
    wide = jnp.broadcast_to(column, (size, size))
    return jnp.sum(jnp.where(eye(size), wide, 0.0), axis=0, keepdims=True)


def to_rows(lanes):
    size = lanes.shape[1]
    wide = jnp.broadcast_to(lanes, (size, size))
    return jnp.sum(jnp.where(eye(size), wide, 0.0), axis=1, keepdims=True)


def join_lse(parts):
    peak = functools.reduce(jnp.maximum, parts)
    total = functools.reduce(jnp.add, [jnp.exp(part - peak) for part in parts])
    return peak + jnp.log(total)


def row_stats(cost_ref, col_pot, inverse):
    tiles = cost_ref.shape[1] // 128

    def score(tile):
        part = cost_ref[:, tile * 128 : (tile + 1) * 128]
        if col_pot is None:
            return -part * inverse
        return (col_pot[tile : tile + 1, :] - part) * inverse

    peak = score(0)
    for tile in range(1, tiles):
        peak = jnp.maximum(peak, score(tile))
    peak = jnp.max(peak, axis=1, keepdims=True)
    return score, peak


def row_lse(cost_ref, col_pot, inverse):
    score, peak = row_stats(cost_ref, col_pot, inverse)
    total = jnp.exp(score(0) - peak)
    for tile in range(1, cost_ref.shape[1] // 128):
        total = total + jnp.exp(score(tile) - peak)
    return peak + jnp.log(jnp.sum(total, axis=1, keepdims=True))


def pack(lse, out_ref):
    place = lax.broadcasted_iota(jnp.int32, (8, 128), 0)
    packed = jnp.zeros((8, 128), F32)
    for part in range(lse.shape[0] // 128):
        packed = jnp.where(place == part, to_lanes(lse[part * 128 : part * 128 + 128]), packed)
    out_ref[...] = jnp.broadcast_to(packed[None], out_ref.shape)


def spread_lse(parts):
    peak = jnp.max(parts, axis=0)
    return peak + jnp.log(jnp.sum(jnp.exp(parts - peak[None]), axis=0))


def square_sum(value):
    total = jnp.zeros((value.shape[0], 128), F32)
    for tile in range(value.shape[1] // 128):
        part = value[:, tile * 128 : (tile + 1) * 128].astype(F32)
        total = total + part * part
    return jnp.sum(total, axis=1, keepdims=True)


def noise_kernel(place, a, b, c, d, noise_ref, square_ref):
    h = place[2]
    rows, latent = a.shape[1:]
    for k, pair in enumerate((a, b, c, d)):
        noise_ref[h ^ (2 * k)] = pair[0]
        noise_ref[h ^ (2 * k + 1)] = pair[1]
    squares = square_sum(noise_ref[...].reshape(8 * rows, latent))
    square_ref[...] = jnp.broadcast_to(squares, square_ref.shape)


def cost_kernel(data_ref, noise_ref, square_ref, cost_ref, lse_ref):
    rows, latent = noise_ref.shape[1:]
    noise = noise_ref[...].reshape(8 * rows, latent)

    for group in range(2):
        part = data_ref[group * 8 : group * 8 + 8].reshape(8 * rows, latent)
        cross = lax.dot_general(
            noise, part, (((1,), (1,)), ((), ())), preferred_element_type=F32
        )
        for side in range(2):
            data_sq = to_lanes(square_sum(part[side * 128 : side * 128 + 128]))
            at = group * 256 + side * 128
            cost_ref[:, at : at + 128] = (
                square_ref[...] + data_sq - 2.0 * cross[:, side * 128 : side * 128 + 128]
            ) / latent
    pack(row_lse(cost_ref, None, 1.0 / epsilon_of(0)), lse_ref)


def col_kernel(step, cost_ref, parts_ref, out_ref):
    epsilon = epsilon_of(step)
    joined = -epsilon * spread_lse(parts_ref[...])
    halfway = cost_ref.shape[0] // 2
    inverse = 1.0 / epsilon
    upper = (to_rows(joined[0:1, :]) - cost_ref[0:halfway, :]) * inverse
    lower = (to_rows(joined[1:2, :]) - cost_ref[halfway : 2 * halfway, :]) * inverse
    peak = jnp.maximum(
        jnp.max(upper, axis=0, keepdims=True), jnp.max(lower, axis=0, keepdims=True)
    )
    total = jnp.sum(jnp.exp(upper - peak) + jnp.exp(lower - peak), axis=0, keepdims=True)
    lse = peak + jnp.log(total)
    place = lax.broadcasted_iota(jnp.int32, (8, 128), 0)
    packed = jnp.zeros((8, 128), F32)
    for tile in range(lse.shape[1] // 128):
        packed = jnp.where(place == tile, lse[:, tile * 128 : (tile + 1) * 128], packed)
    out_ref[...] = jnp.broadcast_to(packed[None], out_ref.shape)


def col_potential(step, parts_ref):
    return -epsilon_of(step) * spread_lse(parts_ref[...])


def row_kernel(step, cost_ref, parts_ref, lse_ref):
    pack(row_lse(cost_ref, col_potential(step - 1, parts_ref), 1.0 / epsilon_of(step)), lse_ref)


def packed_log(value):
    lane = lax.broadcasted_iota(jnp.int32, value.shape, 1)
    high = value.astype(BF).astype(F32)
    middle = (value - high).astype(BF).astype(F32)
    low = value - high - middle
    return jnp.where(
        lane == 0, high, jnp.where(lane == 1, middle, jnp.where(lane == 2, low, 0.0))
    ).astype(BF)


def target_kernel(place, cost_ref, data_ref, parts_ref, keep_ref, log_ref, far_ref, send_ref, coupling, sums, lses):
    h = place[2]
    col_pot = col_potential(ITERS - 1, parts_ref)
    score, peak = row_stats(cost_ref, col_pot, 1.0 / epsilon_of(ITERS - 1))
    total = jnp.zeros(cost_ref.shape[:1] + (128,), F32)
    for tile in range(cost_ref.shape[1] // 128):
        expo = jnp.exp(score(tile) - peak)
        total = total + expo
        coupling[:, tile * 128 : (tile + 1) * 128] = expo.astype(BF)
    denom = jnp.sum(total, axis=1, keepdims=True)
    count, rows, latent = sums.shape
    lses[...] = jnp.broadcast_to(peak + jnp.log(denom), (count * rows, 128)).reshape(lses.shape)
    share = 1.0 / denom
    for at in range(0, latent, 512):
        part = data_ref[:, :, at : at + 512].reshape(-1, 512)
        product = jnp.dot(coupling[...], part, preferred_element_type=F32) * share
        sums[:, :, at : at + 512] = product.reshape(count, rows, 512)
    for k in range(4):
        keep_ref[k] = sums[h ^ (2 * k)]
        log_ref[k] = lses[h ^ (2 * k)]
        out = far_ref if k == 2 else send_ref.at[min(k, 2)]
        out[:, 0:latent] = sums[h ^ (2 * k + 1)].astype(BF)
        out[:, latent : latent + 128] = packed_log(lses[h ^ (2 * k + 1)])


def read_log(ref_value):
    return jnp.sum(ref_value.astype(F32), axis=1, keepdims=True)


def pair_parts(keep_ref, log_ref, got_ref, k):
    latent = keep_ref.shape[2]
    first = log_ref[k]
    second = jnp.broadcast_to(read_log(got_ref[:, latent : latent + 128]), first.shape)
    total = join_lse([first, second])
    mixed = keep_ref[k] * jnp.exp(first - total)[:, 0:1] + got_ref[:, 0:latent].astype(F32) * jnp.exp(second - total)[:, 0:1]
    return mixed, total


def pair_send(keep_ref, log_ref, got_ref, k, out):
    latent = keep_ref.shape[2]
    mixed, total = pair_parts(keep_ref, log_ref, got_ref, k)
    out[:, 0:latent] = mixed.astype(BF)
    out[:, latent : latent + 128] = packed_log(total)


def far_kernel(keep_ref, log_ref, got_ref, out):
    pair_send(keep_ref, log_ref, got_ref, 2, out)


def pair_kernel(keep_ref, log_ref, got_ref, own_ref, own_log_ref, s1, s3):
    own_ref[...], own_log_ref[...] = pair_parts(keep_ref, log_ref, got_ref.at[0], 0)
    pair_send(keep_ref, log_ref, got_ref.at[1], 1, s1)
    pair_send(keep_ref, log_ref, got_ref.at[2], 3, s3)


def spread_kernel(value_ref, out_ref, sems):
    copies = [
        pltpu.make_async_copy(value_ref, out_ref.at[k], sems.at[k])
        for k in range(out_ref.shape[0])
    ]
    for copy in copies:
        copy.start()
    for copy in copies:
        copy.wait()


def qkv_kernel(
    place, own_ref, log_ref, noise_ref, time_ref, table_ref, *refs
):
    far = refs[:7]
    out_ref, velocity_ref, tokens = refs[7:10]
    a, b, c, folded, sems = refs[10:15]
    rows, latent = own_ref.shape
    step = pl.program_id(0)

    @pl.when(step == 0)
    def _():
        copies = [
            pltpu.make_async_copy(there, here, sems.at[k])
            for k, (there, here) in enumerate(zip(far, (a, b, c)))
        ]
        for k in range(16):
            columns = folded.shape[1] // 16
            to = pl.multiple_of((place[3] ^ k) * columns, 128)
            copies.append(
                pltpu.make_async_copy(
                    far[3 + k // 4].at[:, pl.ds((k % 4) * columns, columns)],
                    folded.at[:, pl.ds(to, columns)],
                    sems.at[3 + k],
                )
            )
        for copy in copies:
            copy.start()
        for copy in copies[:3]:
            copy.wait()
        logs = [log_ref[...]] + [
            jnp.broadcast_to(read_log(got[:, latent : latent + 128]), log_ref.shape)
            for got in (a, b, c)
        ]
        total = join_lse(logs)
        shares = [jnp.exp(log - total) for log in logs]
        times = jnp.broadcast_to(time_ref[...].astype(F32) / TGRID, (rows, 128))
        first = lax.broadcasted_iota(jnp.int32, (rows, 128), 1) < 64
        for tile in range(latent // 128):
            cut = slice(tile * 128, tile * 128 + 128)
            target = own_ref[:, cut] * shares[0]
            for got, share in zip((a, b, c), shares[1:]):
                target = target + got[:, cut].astype(F32) * share
            noise = noise_ref[:, cut].astype(F32)
            velocity_ref[:, cut] = (target - noise).astype(BF)
            mixed = ((1.0 - times) * noise + times * target).astype(BF).astype(F32)
            turned = pltpu.roll(mixed, 64, 1)
            tokens[pl.ds(2 * tile, rows, stride=latent // 64), :] = jnp.where(
                first, mixed, turned
            )
            tokens[pl.ds(2 * tile + 1, rows, stride=latent // 64), :] = jnp.where(
                first, turned, mixed
            )
        for copy in copies[3:]:
            copy.wait()

    count = out_ref.shape[0]
    width = table_ref.shape[1]
    patches = tokens[pl.ds(pl.multiple_of(step * count, count), count), :].astype(BF)
    spot = lax.broadcasted_iota(jnp.int32, (count, 128), 0) % 32
    lane = lax.broadcasted_iota(jnp.int32, (count, 128), 1)
    spots = jnp.where(spot == lane % 32, 1.0, 0.0).astype(BF)
    chunk = jnp.concatenate([patches, spots[:, 0:64]], axis=1)
    total = jnp.zeros((count, 128), F32)
    for col in range(0, width, 256):
        part = jnp.dot(chunk, table_ref[:, col : col + 256], preferred_element_type=F32)
        part = part * part
        total = total + part[:, 0:128] + part[:, 128:256]
    scale = lax.rsqrt(jnp.sum(total, axis=1, keepdims=True) / width + 1e-06)
    for at in range(0, folded.shape[1], TILE):
        product = jnp.dot(chunk, folded[:, at : at + TILE], preferred_element_type=F32)
        out_ref[:, at : at + TILE] = (product * scale).astype(BF)


def halves(value):
    high = value.astype(BF)
    low = (value - high.astype(F32)).astype(BF)
    return high, low


def folded_weights(embed_weight, position, norm_gain, qkv_weight):
    scaled = jnp.concatenate([embed_weight, position], 0).astype(F32) * norm_gain
    high, low = halves(scaled)
    both = jnp.dot(jnp.concatenate([high, low], 0), qkv_weight, preferred_element_type=F32)
    rows = scaled.shape[0]
    high, low = halves(both[:rows] + both[rows:])
    split = embed_weight.shape[0]
    return jnp.concatenate([high[:split], low[:split], high[split:], low[split:]], 0)


def together(*values):
    return lax.optimization_barrier(values)


def coupled_target(noise, data, place, folded):
    rows, latent = noise.shape
    noise_pair = jnp.stack([noise, swap(noise, CORE)])
    noises = [noise_pair] + [swap(noise_pair, mask) for mask in Z_STEPS]
    spread = pl.pallas_call(
        spread_kernel,
        out_shape=shape((16, rows, latent), BF),
        in_specs=[pl.BlockSpec(memory_space=pltpu.VMEM)],
        out_specs=pl.BlockSpec(memory_space=pl.ANY),
        scratch_shapes=[pltpu.SemaphoreType.DMA((16,))],
    )(data)
    data_all = exchange(spread, COL_MASK)
    flops = 2 * 8 * rows * 16 * rows * latent
    noise_all, squares = vmem_call(
        noise_kernel,
        (shape((8, rows, latent), BF), shape((8 * rows, 128))),
        smem=1,
        inputs=4,
        nbytes=2 * 1024 * 1024,
    )(place, *noises)
    cost, row_part = vmem_call(
        cost_kernel,
        (shape((8 * rows, 16 * rows)), shape((8, 8, 128))),
        inputs=3,
        flops=flops,
        nbytes=4 * 1024 * 1024,
    )(data_all, noise_all, squares)
    quads = [None] * 4
    folded, row_part = together(folded, row_part)
    folded = jnp.concatenate([folded, swap(folded, CORE)], 1)
    for step in range(ITERS):
        if step == 1:
            folded, row_part = together(folded, row_part)
            quads = [folded, swap(folded, Y_STEPS[0]), None, swap(folded, Y_STEPS[2])]
        elif step == 2:
            folded, row_part = together(folded, row_part)
            quads[2] = swap(folded, Y_STEPS[1])
        row_parts = exchange(row_part, ROW_MASK)
        col_part = vmem_call(
            functools.partial(col_kernel, step), shape((16, 8, 128)), inputs=2, nbytes=1024 * 1024
        )(cost, row_parts)
        if step == 0:
            folded, col_part = together(folded, col_part)
            folded = jnp.concatenate([folded, swap(folded, Z_STEPS[0])], 1)
        col_parts = exchange(col_part, COL_MASK)
        if step == 0:
            folded, col_parts = together(folded, col_parts)
        elif step == 1:
            quads[1], quads[3], col_parts = together(quads[1], quads[3], col_parts)
        elif step == 2:
            quads[2], col_parts = together(quads[2], col_parts)
        if step + 1 < ITERS:
            row_part = vmem_call(
                functools.partial(row_kernel, step + 1),
                shape((8, 8, 128)),
                inputs=2,
                nbytes=1024 * 1024,
            )(cost, col_parts)
    keep, log, first, send = vmem_call(
        target_kernel,
        (
            shape((4, rows, latent)),
            shape((4, rows, 128)),
            shape((rows, latent + 128), BF),
            shape((3, rows, latent + 128), BF),
        ),
        scratch=[
            pltpu.VMEM((8 * rows, 16 * rows), BF),
            pltpu.VMEM((8, rows, latent), F32),
            pltpu.VMEM((8, rows, 128), F32),
        ],
        smem=1,
        inputs=3,
        flops=flops,
        nbytes=6 * 1024 * 1024,
    )(place, cost, data_all, col_parts)
    got_far, got = swap(first, CORE), swap(send, CORE)
    message = shape((rows, latent + 128), BF)
    far_send = vmem_call(far_kernel, message, inputs=3, nbytes=1024 * 1024)(keep, log, got_far)
    far_send, keep = together(far_send, keep)
    own, own_log, *sends = vmem_call(
        pair_kernel,
        (shape((rows, latent)), shape((rows, 128)), message, message),
        inputs=3,
        nbytes=2 * 1024 * 1024,
    )(keep, log, got)
    others = [swap(sends[0], Z_STEPS[0]), swap(far_send, Z_STEPS[1]), swap(sends[1], Z_STEPS[2])]
    return [own, own_log] + others, quads


def local(noise, data, t_index, embed_weight, position, norm_gain, qkv_weight):
    own = noise.shape[0]
    src, tgt = lax.axis_index("src"), lax.axis_index("tgt")
    ring = (src % 2) * 4 + tgt % 4
    place = jnp.stack([src // 2, tgt // 4, ring, tgt]).astype(jnp.int32)
    folded = folded_weights(embed_weight, position, norm_gain, qkv_weight)
    parts, quads = coupled_target(noise, data, place, folded)
    split, width = embed_weight.shape
    patch_count = position.shape[0]
    table = jnp.concatenate(
        [embed_weight, jnp.zeros_like(embed_weight), position, jnp.zeros_like(position)], 0
    )
    depth, columns = quads[0].shape
    columns = 4 * columns
    chunk = 256
    values = [*parts[:2], noise, t_index[:, None], table]
    far = [*parts[2:], *quads]
    qkv, velocity = pl.pallas_call(
        qkv_kernel,
        out_shape=(shape((own * patch_count, columns), BF), shape(noise.shape, BF)),
        grid_spec=pltpu.PrefetchScalarGridSpec(
            num_scalar_prefetch=1,
            grid=(own * patch_count // chunk,),
            in_specs=[pl.BlockSpec(value.shape, lambda j, where: (0, 0)) for value in values]
            + [pl.BlockSpec(memory_space=pltpu.HBM)] * len(far),
            out_specs=(
                pl.BlockSpec((chunk, columns), lambda j, where: (j, 0)),
                pl.BlockSpec(noise.shape, lambda j, where: (0, 0)),
            ),
            scratch_shapes=[pltpu.VMEM((own * patch_count, 2 * split), F32)]
            + [pltpu.VMEM(value.shape, BF) for value in far[:3]]
            + [pltpu.VMEM((depth, columns), BF), pltpu.SemaphoreType.DMA((19,))],
        ),
        compiler_params=pltpu.CompilerParams(vmem_limit_bytes=53 * 1024 * 1024),
        cost_estimate=pl.CostEstimate(
            flops=2 * own * patch_count * depth * columns,
            bytes_accessed=16 * 1024 * 1024,
            transcendentals=0,
        ),
    )(place, *values, *far)
    return (velocity, qkv)


def solution(mesh):
    return jax.shard_map(
        local,
        mesh=mesh,
        in_specs=(
            P(("src", "tgt"), None),
            P(("src", "tgt"), None),
            P(("src", "tgt")),
            P(),
            P(),
            P(),
            P(None, "tgt"),
        ),
        out_specs=(P(("src", "tgt"), None), P(("src", "tgt"), None)),
        check_vma=False,
    )
```
